32 devices in a mesh: task: 2 (over y), fsdp: 16 (over z, x, core).
Axes of the slice: x: 2, y: 2, z: 4, core: 2. Of those that a mesh axis runs over, the one named last changes fastest.
Arguments:
- contexts: bfloat16 [2, 3072, 4096], P('task', 'fsdp'), may hold values from -3400 to 3400
- cotangents: bfloat16 [2, 3072, 4096], P('task', 'fsdp'), may hold values from -3400 to 3400
- adapter: bfloat16 [4096, 256], P('fsdp'), may hold values from -0.09375 to 0.09375
- moment_one: float32 [4096, 256], P('fsdp', 'task'), may hold values from -6 to 6
- moment_two: float32 [4096, 256], P('fsdp', 'task'), may hold values from 0.01 to 10
Outputs:
- first_moment: float32 [4096, 256], P('fsdp', 'task')
- second_moment: float32 [4096, 256], P('fsdp', 'task')
- adam_step: float32 [4096, 256], P('fsdp', 'task')
The draws below stay inside these ranges and needn't reach their ends.
All inputs are finite; a program needn't handle non-finite values.
Results may differ from the reference program's by a relative error of at most 0.0004.
The reference program's roundings to bfloat16 on the way (of `low` and `back`) count: a program that leaves them out, or rounds other values in their place, can miss the bound.
Values may be sent and summed in bfloat16 or wider, within the bound.
A program may use at most 64 MiB of HBM per device.

```python
import math
import jax
import jax.numpy as jnp
from jax import lax

D = 4096
INNER = 4096
RANK = 128
TOKENS = 3072
TASKS = 2


def scaled_field(key, width):
    keys = jax.random.split(key, 4)
    ramp = jnp.arange(width, dtype=jnp.float32) / float(width - 1)
    feature_scale = jnp.exp(math.log(10.0) * ramp) * jax.random.uniform(keys[0], (width,), jnp.float32, 0.7, 1.4)
    token_scale = jnp.exp(jax.random.uniform(keys[1], (TASKS, TOKENS, 1), jnp.float32, 0.0, math.log(10.0)))
    task_scale = jnp.exp(jax.random.uniform(keys[2], (TASKS, 1, 1), jnp.float32, 0.0, math.log(4.0)))
    noise = jax.random.truncated_normal(keys[3], -6.0, 6.0, (TASKS, TOKENS, width), jnp.float32)
    return (noise * token_scale * task_scale * feature_scale).astype(jnp.bfloat16)


def draw_contexts(key, part):
    return scaled_field(jax.random.fold_in(key, 11), INNER)


def draw_cotangents(key, part):
    return scaled_field(jax.random.fold_in(key, 23), D)


def levels(key, shape, cuts, low, top_value):
    def one(dim, parts):
        heights = jax.random.uniform(jax.random.fold_in(jax.random.fold_in(key, 6), dim), (parts,), jnp.float32, low / len(cuts), top_value / len(cuts))
        return jnp.repeat(jnp.exp(heights), shape[dim] // parts).reshape((-1,) + (1,) * (len(shape) - dim - 1))

    level = one(*cuts[0])
    for cut in cuts[1:]:
        level = level * one(*cut)
    return level


def bell_draw(stream_key, shape, deviation, bound, pieces=(), kind=jnp.bfloat16):
    array = deviation * jax.random.normal(stream_key, shape, jnp.float32)
    if pieces:
        array = array * levels(stream_key, shape, pieces, -0.22, 0.18)
    return jnp.clip(array, -bound, bound).astype(kind)


def setup_inputs(seed: int = 0) -> dict:
    key_list = jax.random.split(jax.random.key(seed), 6)
    contexts = draw_contexts(jax.random.fold_in(key_list[5], 71), 0)
    cotangents = draw_cotangents(jax.random.fold_in(key_list[5], 71), 0)
    adapter = bell_draw(key_list[2], (D, 2 * RANK), D ** -0.5, 0.09375, ((0, 16),))
    moment_one = bell_draw(key_list[3], (D, 2 * RANK), 1.0, 6.0, ((0, 16), (1, 2)), jnp.float32)
    moment_two = jnp.clip(jnp.exp(math.log(10.0) - 6.9077553 * jax.random.uniform(key_list[4], (D, 2 * RANK), jnp.float32) ** levels(key_list[4], (D, 2 * RANK), ((0, 16), (1, 2)), -0.2, 0.2)), 0.01, 10.0)
    return {"contexts": contexts, "cotangents": cotangents, "adapter": adapter, "moment_one": moment_one, "moment_two": moment_two}


def eliminate(matrix, vector):
    extent = vector.shape[0]
    matrix_rows = [matrix[position] for position in range(extent)]
    values = [vector[position] for position in range(extent)]
    for column in range(extent):
        for target in range(column + 1, extent):
            factor = matrix_rows[target][column] / matrix_rows[column][column]
            matrix_rows[target] = matrix_rows[target] - factor * matrix_rows[column]
            values[target] = values[target] - factor * values[column]
    answer = [values[0] for position in range(extent)]
    for column in reversed(range(extent)):
        running = values[column]
        for follow in range(column + 1, extent):
            running = running - matrix_rows[column][follow] * answer[follow]
        answer[column] = running / matrix_rows[column][column]
    return jnp.stack(answer)

def task_weights(gram_matrix):
    task_norms = jnp.sqrt(jnp.diagonal(gram_matrix))
    right_side = gram_matrix[0, 0] / task_norms[0] - gram_matrix[0, 1:] / task_norms[1:]
    system = (gram_matrix[0, 0] - gram_matrix[1:, 0])[:, None] / task_norms[0] - (gram_matrix[0, 1:][None, :] - gram_matrix[1:, 1:]) / task_norms[1:][None, :]
    solution = eliminate(system.T, right_side)
    return jnp.concatenate([jnp.reshape(1.0 - jnp.sum(solution), (1,)), solution])

def adam_update(combined, grad_norm, moment_one, moment_two):
    clipped = combined * (math.sqrt(2 * RANK * D) / grad_norm)
    first_moment = 0.9 * moment_one + 0.1 * clipped
    second_moment = 0.95 * moment_two + 0.05 * clipped * clipped
    adam_step = first_moment / (1.0 - 0.9 ** 20) / (jnp.sqrt(second_moment / (1.0 - 0.95 ** 20)) + 1e-08)
    return (first_moment, second_moment, adam_step)

def reference(contexts, cotangents, adapter, moment_one, moment_two):

    def one_task(tensor_pair):
        context_rows, cotangent_rows = tensor_pair
        low = jnp.dot(context_rows, adapter[:, :RANK], preferred_element_type=jnp.float32).astype(adapter.dtype)
        back = jnp.dot(cotangent_rows, adapter[:, RANK:], preferred_element_type=jnp.float32).astype(adapter.dtype)
        down_grad = jnp.dot(context_rows.T, back, preferred_element_type=jnp.float32)
        up_grad = jnp.dot(cotangent_rows.T, low, preferred_element_type=jnp.float32)
        return jnp.concatenate([down_grad, up_grad], axis=1)
    grads = lax.map(one_task, (contexts, cotangents))
    gram_matrix = jnp.einsum('sij,tij->st', grads, grads, precision=lax.Precision.HIGHEST)
    task_alpha = task_weights(gram_matrix)
    combined = jnp.einsum('t,tij->ij', task_alpha, grads, precision=lax.Precision.HIGHEST)
    grad_norm = jnp.sqrt(1e-06 + jnp.sum(combined * combined))
    first_moment, second_moment, adam_step = adam_update(combined, grad_norm, moment_one, moment_two)
    return (first_moment, second_moment, adam_step)
```

```python
import math

import jax
import jax.numpy as jnp
from jax import lax
from jax.experimental import pallas as pl
from jax.experimental.pallas import tpu as pltpu
from jax.sharding import PartitionSpec as P

D = 4096
RANK = 128
MESH = pl.DeviceIdType.MESH


def eliminate(matrix, vector):
    extent = vector.shape[0]
    matrix_rows = [matrix[position] for position in range(extent)]
    values = [vector[position] for position in range(extent)]
    for column in range(extent):
        for target in range(column + 1, extent):
            factor = matrix_rows[target][column] / matrix_rows[column][column]
            matrix_rows[target] = matrix_rows[target] - factor * matrix_rows[column]
            values[target] = values[target] - factor * values[column]
    answer = [values[0] for position in range(extent)]
    for column in reversed(range(extent)):
        running = values[column]
        for follow in range(column + 1, extent):
            running = running - matrix_rows[column][follow] * answer[follow]
        answer[column] = running / matrix_rows[column][column]
    return jnp.stack(answer)


def task_weights(gram_matrix):
    task_norms = jnp.sqrt(jnp.diagonal(gram_matrix))
    right_side = gram_matrix[0, 0] / task_norms[0] - gram_matrix[0, 1:] / task_norms[1:]
    system = (gram_matrix[0, 0] - gram_matrix[1:, 0])[:, None] / task_norms[0] - (
        gram_matrix[0, 1:][None, :] - gram_matrix[1:, 1:]
    ) / task_norms[1:][None, :]
    solution = eliminate(system.T, right_side)
    return jnp.concatenate([jnp.reshape(1.0 - jnp.sum(solution), (1,)), solution])


def adam(clipped, moment_one, moment_two):
    first_moment = 0.9 * moment_one + 0.1 * clipped
    second_moment = 0.95 * moment_two + 0.05 * clipped * clipped
    adam_step = (
        first_moment / (1.0 - 0.9**20) / (jnp.sqrt(second_moment / (1.0 - 0.95**20)) + 1e-08)
    )
    return (first_moment, second_moment, adam_step)


def general_body(contexts, cotangents, adapter, moment_one, moment_two):
    own_context = contexts[0]
    own_cotangent = cotangents[0]
    rank_width = adapter.shape[1] // 2
    piece = lax.all_gather(adapter, "fsdp", axis=0, tiled=True)
    low = jnp.dot(own_context, piece[:, :rank_width], preferred_element_type=jnp.float32)
    back = jnp.dot(own_cotangent, piece[:, rank_width:], preferred_element_type=jnp.float32)
    low = low.astype(jnp.bfloat16)
    back = back.astype(jnp.bfloat16)
    over_tokens = (((0,), (0,)), ((), ()))
    down_part = lax.dot_general(own_context, back, over_tokens, preferred_element_type=jnp.float32)
    up_part = lax.dot_general(own_cotangent, low, over_tokens, preferred_element_type=jnp.float32)
    grad_rows = lax.psum_scatter(
        jnp.concatenate([down_part, up_part], axis=1), "fsdp", scatter_dimension=0, tiled=True
    )
    gathered = lax.all_gather(grad_rows[None], "task", axis=0, tiled=True)
    partial_gram = jnp.einsum("sij,tij->st", gathered, gathered, precision=lax.Precision.HIGHEST)
    gram_matrix = lax.psum(partial_gram, "fsdp")
    block_width = gathered.shape[2] // lax.axis_size("task")
    pieces = lax.dynamic_slice_in_dim(
        gathered, lax.axis_index("task") * block_width, block_width, 2
    )
    task_alpha = task_weights(gram_matrix)
    combined = jnp.einsum("t,tij->ij", task_alpha, pieces, precision=lax.Precision.HIGHEST)
    squared = lax.psum(jnp.sum(combined * combined), ("task", "fsdp"))
    grad_norm = jnp.sqrt(1e-06 + squared)
    clipped = combined * (math.sqrt(2 * RANK * D) / grad_norm)
    return adam(clipped, moment_one, moment_two)


def flip2(z, d):
    if d == 0:
        return z
    if d == 1:
        return z + 1 - 2 * (z % 2)
    if d == 2:
        return (z + 2) % 4
    return 3 - z


def kernel(
    ctx, cot, ada, out,
    gathered, grad, core_in, x_in, z_in, y_in, gram_out, gram_in, gram_mid, gram_last,
    az_s, az_r, ax_s, ax_r, ac_s, ac_r,
    gc_s, gc_r, gx_s, gx_r, gz_s, gz_r, gy_s, gy_r, ka_s, ka_r, kz_s, kz_r,
):
    f32 = jnp.float32
    rows, width = ada.shape
    rank = width // 2
    t = lax.axis_index("task")
    f = lax.axis_index("fsdp")
    c = f % 2
    x = (f // 2) % 2
    z = f // 4

    def place(z_, x_, c_):
        return (z_ * 2 + x_) * 2 + c_

    zpeer = {d: (t, place(flip2(z, d), x, c)) for d in (1, 2, 3)}
    xpeer = (t, place(z, 1 - x, c))
    cpeer = (t, place(z, x, 1 - c))
    cube = {
        k: (
            1 - t if k & 4 else t,
            place(z, 1 - x if k & 2 else x, 1 - c if k & 1 else c),
        )
        for k in range(1, 8)
    }

    def remote(src, dst, send, recv, peer):
        return pltpu.make_async_remote_copy(
            src_ref=src, dst_ref=dst, send_sem=send, recv_sem=recv, device_id=peer, device_id_type=MESH
        )

    barrier = pltpu.get_barrier_semaphore()
    for peer in list(zpeer.values()) + list(cube.values()):
        pl.semaphore_signal(barrier, inc=1, device_id=peer, device_id_type=MESH)
    gathered[f] = ada[...]
    pl.semaphore_wait(barrier, 10)

    sent = []

    def go(src, dst, send, recv, peer):
        copy = remote(src, dst, send, recv, peer)
        copy.start()
        sent.append(copy)

    def move_block(slot, send, recv, peer):
        go(gathered.at[slot], gathered.at[slot], send, recv, peer)

    def await_block(slot, send, recv, peer):
        remote(gathered.at[slot], gathered.at[slot], send, recv, peer).wait_recv()

    low = jnp.zeros((ctx.shape[0], rank), f32)
    back = jnp.zeros((ctx.shape[0], rank), f32)

    def columns(slot):
        return pl.ds(pl.multiple_of(slot * rows, rows), rows)

    def consume(slot, low, back):
        cols = columns(slot)
        low = low + jnp.dot(ctx[:, cols], gathered[slot, :, :rank], preferred_element_type=f32)
        back = back + jnp.dot(cot[:, cols], gathered[slot, :, rank:], preferred_element_type=f32)
        return low, back

    for d in (3, 2, 1):
        move_block(f, az_s.at[d], az_r.at[d], zpeer[d])
    move_block(f, ax_s.at[0], ax_r.at[0], xpeer)
    move_block(f, ac_s.at[0], ac_r.at[0], cpeer)
    low, back = consume(f, low, back)
    for d in (1, 2, 3):
        slot = place(flip2(z, d), x, c)
        await_block(slot, az_s.at[d], az_r.at[d], zpeer[d])
        move_block(slot, ax_s.at[d], ax_r.at[d], xpeer)
        move_block(slot, ac_s.at[d], ac_r.at[d], cpeer)
        low, back = consume(slot, low, back)
    for d in range(4):
        slot = place(flip2(z, d), 1 - x, c)
        await_block(slot, ax_s.at[d], ax_r.at[d], xpeer)
        move_block(slot, ac_s.at[4 + d], ac_r.at[4 + d], cpeer)
        low, back = consume(slot, low, back)
    for k in range(8):
        slot = place(flip2(z, k % 4), x if k < 4 else 1 - x, 1 - c)
        await_block(slot, ac_s.at[k], ac_r.at[k], cpeer)
        low, back = consume(slot, low, back)

    low_t = low.T.astype(jnp.bfloat16)
    back_t = back.T.astype(jnp.bfloat16)

    def make(slot):
        cols = columns(slot)
        grad[slot, :rank, :] = jnp.dot(back_t, ctx[:, cols], preferred_element_type=f32)
        grad[slot, rank:, :] = jnp.dot(low_t, cot[:, cols], preferred_element_type=f32)

    order = (3, 2, 1, 0)

    def to_core(d, far):
        slot = place(flip2(z, d), 1 - x if far else x, 1 - c)
        make(slot)
        k = 4 * far + d
        go(grad.at[slot], core_in.at[k], gc_s.at[k], gc_r.at[k], cpeer)

    def keep(d, far):
        make(place(flip2(z, d), 1 - x if far else x, c))

    def add_core(d, far):
        slot = place(flip2(z, d), 1 - x if far else x, c)
        k = 4 * far + d
        remote(core_in.at[k], core_in.at[k], gc_s.at[k], gc_r.at[k], cpeer).wait_recv()
        grad[slot] = grad[slot] + core_in[k]
        return slot

    def to_x(d):
        slot = add_core(d, 1)
        go(grad.at[slot], x_in.at[d], gx_s.at[d], gx_r.at[d], xpeer)

    to_core(order[0], 1)
    keep(order[0], 1)
    for before, now in zip(order[:-1], order[1:]):
        to_core(now, 1)
        to_x(before)
        keep(now, 1)
    to_x(order[-1])
    for d in order:
        to_core(d, 0)
        keep(d, 0)
    for d in order:
        slot = add_core(d, 0)
        remote(x_in.at[d], x_in.at[d], gx_s.at[d], gx_r.at[d], xpeer).wait_recv()
        grad[slot] = grad[slot] + x_in[d]
        if d:
            go(grad.at[slot], z_in.at[d - 1], gz_s.at[d], gz_r.at[d], zpeer[d])
    for d in (3, 2, 1):
        remote(z_in.at[d - 1], z_in.at[d - 1], gz_s.at[d], gz_r.at[d], zpeer[d]).wait_recv()
    mine = pl.ds(pl.multiple_of(t * rank, rank), rank)
    theirs = pl.ds(pl.multiple_of((1 - t) * rank, rank), rank)
    for wait in sent:
        wait.wait_send()
    sent.clear()
    z_in[0, theirs, :] = grad[f, theirs, :] + z_in[0, theirs, :] + z_in[1, theirs, :] + z_in[2, theirs, :]
    go(z_in.at[0, theirs, :], y_in, gy_s, gy_r, cube[4])
    own = grad[f, mine, :] + z_in[0, mine, :] + z_in[1, mine, :] + z_in[2, mine, :]
    remote(y_in, y_in, gy_s, gy_r, cube[4]).wait_recv()
    other = y_in[...]

    first = t == 0
    own_sum = jnp.sum(own * own, axis=0, keepdims=True)
    both_sum = jnp.sum(own * other, axis=0, keepdims=True)
    other_sum = jnp.sum(other * other, axis=0, keepdims=True)
    rows_list = [jnp.where(first, own_sum, other_sum), both_sum, jnp.where(first, other_sum, own_sum)]
    gram_out[...] = jnp.zeros_like(gram_out)
    for k in range(3):
        total = rows_list[k]
        acc = total[:, :128]
        for j in range(1, rows // 128):
            acc = acc + total[:, j * 128 : (j + 1) * 128]
        gram_out[k : k + 1, :] = acc
    corner = (t * 2 + x) * 2 + c
    for k in range(1, 8):
        go(gram_out, gram_in.at[corner], ka_s.at[k], ka_r.at[k], cube[k])
    gram_in[corner] = gram_out[...]
    for k in range(1, 8):
        there = ((1 - t if k & 4 else t) * 2 + (1 - x if k & 2 else x)) * 2 + (1 - c if k & 1 else c)
        remote(gram_out, gram_in.at[there], ka_s.at[k], ka_r.at[k], cube[k]).wait_recv()
    gram_mid[...] = jnp.sum(gram_in[...], axis=0)
    for d in (3, 2, 1):
        go(gram_mid, gram_last.at[z], kz_s.at[d], kz_r.at[d], zpeer[d])
    gram_last[z] = gram_mid[...]
    for d in (3, 2, 1):
        remote(gram_mid, gram_last.at[flip2(z, d)], kz_s.at[d], kz_r.at[d], zpeer[d]).wait_recv()
    tile = jnp.sum(gram_last[...], axis=0)
    sums = jnp.sum(tile, axis=1, keepdims=True)
    k00, k01, k11 = sums[0:1], sums[1:2], sums[2:3]
    n0, n1 = jnp.sqrt(k00), jnp.sqrt(k11)
    right_side = k00 / n0 - k01 / n1
    system = (k00 - k01) / n0 - (k01 - k11) / n1
    alpha1 = right_side / system
    alpha0 = 1.0 - alpha1
    squared = alpha0 * alpha0 * k00 + 2.0 * alpha0 * alpha1 * k01 + alpha1 * alpha1 * k11
    scale = math.sqrt(2 * RANK * D) / jnp.sqrt(1e-06 + jnp.maximum(squared, 0.0))
    own_alpha = jnp.where(first, alpha0, alpha1) * scale
    other_alpha = jnp.where(first, alpha1, alpha0) * scale
    out[...] = (own * own_alpha + other * other_alpha).T
    for wait in sent:
        wait.wait_send()


def kernel_body(contexts, cotangents, adapter, moment_one, moment_two):
    rows, width = adapter.shape
    rank = width // 2
    f32 = jnp.float32
    dma = pltpu.SemaphoreType.DMA
    vmem = pl.BlockSpec(memory_space=pltpu.VMEM)
    clipped = pl.pallas_call(
        kernel,
        out_shape=jax.ShapeDtypeStruct((rows, rank), f32),
        in_specs=[vmem] * 3,
        out_specs=vmem,
        scratch_shapes=[
            pltpu.VMEM((16, rows, width), adapter.dtype),
            pltpu.VMEM((16, width, rows), f32),
            pltpu.VMEM((8, width, rows), f32),
            pltpu.VMEM((4, width, rows), f32),
            pltpu.VMEM((3, width, rows), f32),
            pltpu.VMEM((rank, rows), f32),
            pltpu.VMEM((8, 128), f32),
            pltpu.VMEM((8, 8, 128), f32),
            pltpu.VMEM((8, 128), f32),
            pltpu.VMEM((4, 8, 128), f32),
            dma((4,)), dma((4,)), dma((4,)), dma((4,)), dma((8,)), dma((8,)),
            dma((8,)), dma((8,)), dma((4,)), dma((4,)), dma((4,)), dma((4,)),
            dma, dma, dma((8,)), dma((8,)), dma((4,)), dma((4,)),
        ],
        compiler_params=pltpu.CompilerParams(
            collective_id=0, has_side_effects=True, vmem_limit_bytes=40 * 1024 * 1024
        ),
        name="grads_and_weights",
    )(contexts[0], cotangents[0], adapter)
    return adam(clipped, moment_one, moment_two)


def solution(mesh):
    in_specs = (
        P("task", "fsdp", None),
        P("task", "fsdp", None),
        P("fsdp", None),
        P("fsdp", "task"),
        P("fsdp", "task"),
    )
    out_specs = (P("fsdp", "task"), P("fsdp", "task"), P("fsdp", "task"))
    small = mesh.shape["task"] == 2 and mesh.shape["fsdp"] == 16
    body = kernel_body if small else general_body
    return jax.shard_map(body, mesh=mesh, in_specs=in_specs, out_specs=out_specs, check_vma=False)
```

```python
import math

import jax
import jax.numpy as jnp
from jax import lax
from jax.experimental import pallas as pl
from jax.experimental.pallas import tpu as pltpu
from jax.sharding import PartitionSpec as P

D = 4096
RANK = 128
MESH = pl.DeviceIdType.MESH


def eliminate(matrix, vector):
    extent = vector.shape[0]
    matrix_rows = [matrix[position] for position in range(extent)]
    values = [vector[position] for position in range(extent)]
    for column in range(extent):
        for target in range(column + 1, extent):
            factor = matrix_rows[target][column] / matrix_rows[column][column]
            matrix_rows[target] = matrix_rows[target] - factor * matrix_rows[column]
            values[target] = values[target] - factor * values[column]
    answer = [values[0] for position in range(extent)]
    for column in reversed(range(extent)):
        running = values[column]
        for follow in range(column + 1, extent):
            running = running - matrix_rows[column][follow] * answer[follow]
        answer[column] = running / matrix_rows[column][column]
    return jnp.stack(answer)


def task_weights(gram_matrix):
    task_norms = jnp.sqrt(jnp.diagonal(gram_matrix))
    right_side = gram_matrix[0, 0] / task_norms[0] - gram_matrix[0, 1:] / task_norms[1:]
    system = (gram_matrix[0, 0] - gram_matrix[1:, 0])[:, None] / task_norms[0] - (
        gram_matrix[0, 1:][None, :] - gram_matrix[1:, 1:]
    ) / task_norms[1:][None, :]
    solution = eliminate(system.T, right_side)
    return jnp.concatenate([jnp.reshape(1.0 - jnp.sum(solution), (1,)), solution])


def adam(clipped, moment_one, moment_two):
    first_moment = 0.9 * moment_one + 0.1 * clipped
    second_moment = 0.95 * moment_two + 0.05 * clipped * clipped
    adam_step = (
        first_moment / (1.0 - 0.9**20) / (jnp.sqrt(second_moment / (1.0 - 0.95**20)) + 1e-08)
    )
    return (first_moment, second_moment, adam_step)


def general_body(contexts, cotangents, adapter, moment_one, moment_two):
    own_context = contexts[0]
    own_cotangent = cotangents[0]
    rank_width = adapter.shape[1] // 2
    piece = lax.all_gather(adapter, "fsdp", axis=0, tiled=True)
    low = jnp.dot(own_context, piece[:, :rank_width], preferred_element_type=jnp.float32)
    back = jnp.dot(own_cotangent, piece[:, rank_width:], preferred_element_type=jnp.float32)
    low = low.astype(jnp.bfloat16)
    back = back.astype(jnp.bfloat16)
    over_tokens = (((0,), (0,)), ((), ()))
    down_part = lax.dot_general(own_context, back, over_tokens, preferred_element_type=jnp.float32)
    up_part = lax.dot_general(own_cotangent, low, over_tokens, preferred_element_type=jnp.float32)
    grad_rows = lax.psum_scatter(
        jnp.concatenate([down_part, up_part], axis=1), "fsdp", scatter_dimension=0, tiled=True
    )
    gathered = lax.all_gather(grad_rows[None], "task", axis=0, tiled=True)
    partial_gram = jnp.einsum("sij,tij->st", gathered, gathered, precision=lax.Precision.HIGHEST)
    gram_matrix = lax.psum(partial_gram, "fsdp")
    block_width = gathered.shape[2] // lax.axis_size("task")
    pieces = lax.dynamic_slice_in_dim(
        gathered, lax.axis_index("task") * block_width, block_width, 2
    )
    task_alpha = task_weights(gram_matrix)
    combined = jnp.einsum("t,tij->ij", task_alpha, pieces, precision=lax.Precision.HIGHEST)
    squared = lax.psum(jnp.sum(combined * combined), ("task", "fsdp"))
    grad_norm = jnp.sqrt(1e-06 + squared)
    clipped = combined * (math.sqrt(2 * RANK * D) / grad_norm)
    return adam(clipped, moment_one, moment_two)


def flip2(z, d):
    if d == 0:
        return z
    if d == 1:
        return z + 1 - 2 * (z % 2)
    if d == 2:
        return (z + 2) % 4
    return 3 - z


def kernel(
    ctx_hbm, cot_hbm, ada_hbm, out,
    ctx, cot,
    gathered, grad, core_in, x_in, z_in, y_in, gram_out, gram_in, gram_mid, gram_last,
    load, az_s, az_r, ax_s, ax_r, ay_s, ay_r, ac_s, ac_r,
    gc_s, gc_r, gx_s, gx_r, gz_s, gz_r, gy_s, gy_r, ka_s, ka_r, kz_s, kz_r,
):
    f32 = jnp.float32
    rows, width = ada_hbm.shape
    rank = width // 2
    half = rows // 2
    t = lax.axis_index("task")
    f = lax.axis_index("fsdp")
    c = f % 2
    x = (f // 2) % 2
    z = f // 4

    def place(z_, x_, c_):
        return (z_ * 2 + x_) * 2 + c_

    zpeer = {d: (t, place(flip2(z, d), x, c)) for d in (1, 2, 3)}
    xpeer = (t, place(z, 1 - x, c))
    cpeer = (t, place(z, x, 1 - c))
    cube = {
        k: (
            1 - t if k & 4 else t,
            place(z, 1 - x if k & 2 else x, 1 - c if k & 1 else c),
        )
        for k in range(1, 8)
    }

    def remote(src, dst, send, recv, peer):
        return pltpu.make_async_remote_copy(
            src_ref=src, dst_ref=dst, send_sem=send, recv_sem=recv, device_id=peer, device_id_type=MESH
        )

    loads = [
        pltpu.make_async_copy(ada_hbm, gathered.at[f], load.at[0]),
        pltpu.make_async_copy(ctx_hbm, ctx, load.at[1]),
        pltpu.make_async_copy(cot_hbm, cot, load.at[2]),
    ]
    for copy in loads:
        copy.start()
    barrier = pltpu.get_barrier_semaphore()
    for peer in list(zpeer.values()) + list(cube.values()):
        pl.semaphore_signal(barrier, inc=1, device_id=peer, device_id_type=MESH)
    pl.semaphore_wait(barrier, 10)

    sent = []

    def go(src, dst, send, recv, peer):
        copy = remote(src, dst, send, recv, peer)
        copy.start()
        sent.append(copy)

    near_half = pl.ds(pl.multiple_of(t * half, half), half)
    far_half = pl.ds(pl.multiple_of((1 - t) * half, half), half)
    whole = pl.ds(0, rows)
    ypeer = cube[4]

    def move_block(slot, part, send, recv, peer):
        go(gathered.at[slot, part, :], gathered.at[slot, part, :], send, recv, peer)

    def await_block(slot, part, send, recv, peer):
        ref = gathered.at[slot, part, :]
        remote(ref, ref, send, recv, peer).wait_recv()

    low = jnp.zeros((ctx.shape[0], rank), f32)
    back = jnp.zeros((ctx.shape[0], rank), f32)

    def columns(slot):
        return pl.ds(pl.multiple_of(slot * rows, rows), rows)

    def consume(slot, low, back):
        cols = columns(slot)
        low = low + jnp.dot(ctx[:, cols], gathered[slot, :, :rank], preferred_element_type=f32)
        back = back + jnp.dot(cot[:, cols], gathered[slot, :, rank:], preferred_element_type=f32)
        return low, back

    def line(d, far):
        return place(flip2(z, d), 1 - x if far else x, c)

    def to_other_core(slot, part, k):
        move_block(slot, part, ac_s.at[k], ac_r.at[k], cpeer)

    loads[0].wait()
    for d in (3, 2, 1):
        move_block(f, near_half, az_s.at[d], az_r.at[d], zpeer[d])
    move_block(f, whole, ax_s.at[0], ax_r.at[0], xpeer)
    to_other_core(f, whole, 0)
    loads[1].wait()
    loads[2].wait()
    low, back = consume(f, low, back)

    def from_z(d):
        slot = line(d, 0)
        await_block(slot, near_half, az_s.at[d], az_r.at[d], zpeer[d])
        move_block(slot, near_half, ax_s.at[d], ax_r.at[d], xpeer)
        move_block(slot, near_half, ay_s.at[d], ay_r.at[d], ypeer)
        to_other_core(slot, near_half, d)

    from_z(1)
    from_z(2)
    await_block(line(0, 1), whole, ax_s.at[0], ax_r.at[0], xpeer)
    to_other_core(line(0, 1), whole, 4)
    from_z(3)
    low, back = consume(line(0, 1), low, back)
    for d in (1, 2, 3):
        slot = line(d, 1)
        await_block(slot, near_half, ax_s.at[d], ax_r.at[d], xpeer)
        move_block(slot, near_half, ay_s.at[4 + d], ay_r.at[4 + d], ypeer)
        to_other_core(slot, near_half, 4 + d)
    for far in (0, 1):
        slot = place(z, 1 - x if far else x, 1 - c)
        await_block(slot, whole, ac_s.at[4 * far], ac_r.at[4 * far], cpeer)
        low, back = consume(slot, low, back)
    for far in (0, 1):
        for d in (1, 2, 3):
            k = 4 * far + d
            slot = line(d, far)
            await_block(slot, far_half, ay_s.at[k], ay_r.at[k], ypeer)
            to_other_core(slot, far_half, 8 + k)
            low, back = consume(slot, low, back)
    for far in (0, 1):
        for d in (1, 2, 3):
            k = 4 * far + d
            slot = place(flip2(z, d), 1 - x if far else x, 1 - c)
            await_block(slot, near_half, ac_s.at[k], ac_r.at[k], cpeer)
            await_block(slot, far_half, ac_s.at[8 + k], ac_r.at[8 + k], cpeer)
            low, back = consume(slot, low, back)

    low_t = low.T.astype(jnp.bfloat16)
    back_t = back.T.astype(jnp.bfloat16)

    def make(slot):
        cols = columns(slot)
        grad[slot, :rank, :] = jnp.dot(back_t, ctx[:, cols], preferred_element_type=f32)
        grad[slot, rank:, :] = jnp.dot(low_t, cot[:, cols], preferred_element_type=f32)

    order = (2, 3, 1, 0)

    def to_core(d, far):
        slot = place(flip2(z, d), 1 - x if far else x, 1 - c)
        make(slot)
        k = 4 * far + d
        go(grad.at[slot], core_in.at[k], gc_s.at[k], gc_r.at[k], cpeer)

    def keep(d, far):
        make(place(flip2(z, d), 1 - x if far else x, c))

    def add_core(d, far):
        slot = place(flip2(z, d), 1 - x if far else x, c)
        k = 4 * far + d
        remote(core_in.at[k], core_in.at[k], gc_s.at[k], gc_r.at[k], cpeer).wait_recv()
        grad[slot] = grad[slot] + core_in[k]
        return slot

    def to_x(d):
        slot = add_core(d, 1)
        go(grad.at[slot], x_in.at[d], gx_s.at[d], gx_r.at[d], xpeer)

    to_core(order[0], 1)
    keep(order[0], 1)
    for before, now in zip(order[:-1], order[1:]):
        to_core(now, 1)
        to_x(before)
        keep(now, 1)
    to_x(order[-1])
    for d in order:
        to_core(d, 0)
        keep(d, 0)
    for d in order:
        slot = add_core(d, 0)
        remote(x_in.at[d], x_in.at[d], gx_s.at[d], gx_r.at[d], xpeer).wait_recv()
        grad[slot] = grad[slot] + x_in[d]
        if d in (1, 2):
            go(grad.at[slot], z_in.at[d], gz_s.at[d], gz_r.at[d], zpeer[1])
        if d == 3:
            remote(z_in.at[2], z_in.at[2], gz_s.at[2], gz_r.at[2], zpeer[1]).wait_recv()
            grad[slot] = grad[slot] + z_in[2]
            go(grad.at[slot], z_in.at[0], gz_s.at[3], gz_r.at[3], zpeer[3])
    remote(z_in.at[1], z_in.at[1], gz_s.at[1], gz_r.at[1], zpeer[1]).wait_recv()
    remote(z_in.at[0], z_in.at[0], gz_s.at[3], gz_r.at[3], zpeer[3]).wait_recv()
    mine = pl.ds(pl.multiple_of(t * rank, rank), rank)
    theirs = pl.ds(pl.multiple_of((1 - t) * rank, rank), rank)
    z_in[0, theirs, :] = grad[f, theirs, :] + z_in[0, theirs, :] + z_in[1, theirs, :]
    go(z_in.at[0, theirs, :], y_in, gy_s, gy_r, cube[4])
    own = grad[f, mine, :] + z_in[0, mine, :] + z_in[1, mine, :]
    remote(y_in, y_in, gy_s, gy_r, cube[4]).wait_recv()
    other = y_in[...]

    first = t == 0
    own_sum = jnp.sum(own * own, axis=0, keepdims=True)
    both_sum = jnp.sum(own * other, axis=0, keepdims=True)
    other_sum = jnp.sum(other * other, axis=0, keepdims=True)
    rows_list = [jnp.where(first, own_sum, other_sum), both_sum, jnp.where(first, other_sum, own_sum)]
    gram_out[...] = jnp.zeros_like(gram_out)
    for k in range(3):
        total = rows_list[k]
        acc = total[:, :128]
        for j in range(1, rows // 128):
            acc = acc + total[:, j * 128 : (j + 1) * 128]
        gram_out[k : k + 1, :] = acc
    corner = (t * 2 + x) * 2 + c
    for k in range(1, 8):
        go(gram_out, gram_in.at[corner], ka_s.at[k], ka_r.at[k], cube[k])
    gram_in[corner] = gram_out[...]
    for k in range(1, 8):
        there = ((1 - t if k & 4 else t) * 2 + (1 - x if k & 2 else x)) * 2 + (1 - c if k & 1 else c)
        remote(gram_out, gram_in.at[there], ka_s.at[k], ka_r.at[k], cube[k]).wait_recv()
    gram_mid[...] = jnp.sum(gram_in[...], axis=0)
    for d in (3, 2, 1):
        go(gram_mid, gram_last.at[z], kz_s.at[d], kz_r.at[d], zpeer[d])
    gram_last[z] = gram_mid[...]
    for d in (3, 2, 1):
        remote(gram_mid, gram_last.at[flip2(z, d)], kz_s.at[d], kz_r.at[d], zpeer[d]).wait_recv()
    tile = jnp.sum(gram_last[...], axis=0)
    sums = jnp.sum(tile, axis=1, keepdims=True)
    k00, k01, k11 = sums[0:1], sums[1:2], sums[2:3]
    n0, n1 = jnp.sqrt(k00), jnp.sqrt(k11)
    right_side = k00 / n0 - k01 / n1
    system = (k00 - k01) / n0 - (k01 - k11) / n1
    alpha1 = right_side / system
    alpha0 = 1.0 - alpha1
    squared = alpha0 * alpha0 * k00 + 2.0 * alpha0 * alpha1 * k01 + alpha1 * alpha1 * k11
    scale = math.sqrt(2 * RANK * D) / jnp.sqrt(1e-06 + jnp.maximum(squared, 0.0))
    own_alpha = jnp.where(first, alpha0, alpha1) * scale
    other_alpha = jnp.where(first, alpha1, alpha0) * scale
    out[...] = (own * own_alpha + other * other_alpha).T
    for wait in sent:
        wait.wait_send()


def kernel_body(contexts, cotangents, adapter, moment_one, moment_two):
    rows, width = adapter.shape
    rank = width // 2
    f32 = jnp.float32
    dma = pltpu.SemaphoreType.DMA
    vmem = pl.BlockSpec(memory_space=pltpu.VMEM)
    clipped = pl.pallas_call(
        kernel,
        out_shape=jax.ShapeDtypeStruct((rows, rank), f32),
        in_specs=[pl.BlockSpec(memory_space=pltpu.HBM)] * 3,
        out_specs=vmem,
        scratch_shapes=[
            pltpu.VMEM(contexts.shape[1:], contexts.dtype),
            pltpu.VMEM(contexts.shape[1:], contexts.dtype),
            pltpu.VMEM((16, rows, width), adapter.dtype),
            pltpu.VMEM((16, width, rows), f32),
            pltpu.VMEM((8, width, rows), f32),
            pltpu.VMEM((4, width, rows), f32),
            pltpu.VMEM((3, width, rows), f32),
            pltpu.VMEM((rank, rows), f32),
            pltpu.VMEM((8, 128), f32),
            pltpu.VMEM((8, 8, 128), f32),
            pltpu.VMEM((8, 128), f32),
            pltpu.VMEM((4, 8, 128), f32),
            dma((3,)), dma((4,)), dma((4,)), dma((4,)), dma((4,)), dma((8,)), dma((8,)), dma((16,)), dma((16,)),
            dma((8,)), dma((8,)), dma((4,)), dma((4,)), dma((4,)), dma((4,)),
            dma, dma, dma((8,)), dma((8,)), dma((4,)), dma((4,)),
        ],
        compiler_params=pltpu.CompilerParams(
            collective_id=0, has_side_effects=True, vmem_limit_bytes=40 * 1024 * 1024
        ),
        name="grads_and_weights",
    )(contexts[0], cotangents[0], adapter)
    return adam(clipped, moment_one, moment_two)


def solution(mesh):
    in_specs = (
        P("task", "fsdp", None),
        P("task", "fsdp", None),
        P("fsdp", None),
        P("fsdp", "task"),
        P("fsdp", "task"),
    )
    out_specs = (P("fsdp", "task"), P("fsdp", "task"), P("fsdp", "task"))
    small = mesh.shape["task"] == 2 and mesh.shape["fsdp"] == 16
    body = kernel_body if small else general_body
    return jax.shard_map(body, mesh=mesh, in_specs=in_specs, out_specs=out_specs, check_vma=False)
```

```python
import math

import jax
import jax.numpy as jnp
from jax import lax
from jax.experimental import pallas as pl
from jax.experimental.pallas import tpu as pltpu
from jax.sharding import PartitionSpec as P

D = 4096
RANK = 128
MESH = pl.DeviceIdType.MESH


def eliminate(matrix, vector):
    extent = vector.shape[0]
    matrix_rows = [matrix[position] for position in range(extent)]
    values = [vector[position] for position in range(extent)]
    for column in range(extent):
        for target in range(column + 1, extent):
            factor = matrix_rows[target][column] / matrix_rows[column][column]
            matrix_rows[target] = matrix_rows[target] - factor * matrix_rows[column]
            values[target] = values[target] - factor * values[column]
    answer = [values[0] for position in range(extent)]
    for column in reversed(range(extent)):
        running = values[column]
        for follow in range(column + 1, extent):
            running = running - matrix_rows[column][follow] * answer[follow]
        answer[column] = running / matrix_rows[column][column]
    return jnp.stack(answer)


def task_weights(gram_matrix):
    task_norms = jnp.sqrt(jnp.diagonal(gram_matrix))
    right_side = gram_matrix[0, 0] / task_norms[0] - gram_matrix[0, 1:] / task_norms[1:]
    system = (gram_matrix[0, 0] - gram_matrix[1:, 0])[:, None] / task_norms[0] - (
        gram_matrix[0, 1:][None, :] - gram_matrix[1:, 1:]
    ) / task_norms[1:][None, :]
    solution = eliminate(system.T, right_side)
    return jnp.concatenate([jnp.reshape(1.0 - jnp.sum(solution), (1,)), solution])


def adam(clipped, moment_one, moment_two):
    first_moment = 0.9 * moment_one + 0.1 * clipped
    second_moment = 0.95 * moment_two + 0.05 * clipped * clipped
    adam_step = (
        first_moment / (1.0 - 0.9**20) / (jnp.sqrt(second_moment / (1.0 - 0.95**20)) + 1e-08)
    )
    return (first_moment, second_moment, adam_step)


def general_body(contexts, cotangents, adapter, moment_one, moment_two):
    own_context = contexts[0]
    own_cotangent = cotangents[0]
    rank_width = adapter.shape[1] // 2
    piece = lax.all_gather(adapter, "fsdp", axis=0, tiled=True)
    low = jnp.dot(own_context, piece[:, :rank_width], preferred_element_type=jnp.float32)
    back = jnp.dot(own_cotangent, piece[:, rank_width:], preferred_element_type=jnp.float32)
    low = low.astype(jnp.bfloat16)
    back = back.astype(jnp.bfloat16)
    over_tokens = (((0,), (0,)), ((), ()))
    down_part = lax.dot_general(own_context, back, over_tokens, preferred_element_type=jnp.float32)
    up_part = lax.dot_general(own_cotangent, low, over_tokens, preferred_element_type=jnp.float32)
    grad_rows = lax.psum_scatter(
        jnp.concatenate([down_part, up_part], axis=1), "fsdp", scatter_dimension=0, tiled=True
    )
    gathered = lax.all_gather(grad_rows[None], "task", axis=0, tiled=True)
    partial_gram = jnp.einsum("sij,tij->st", gathered, gathered, precision=lax.Precision.HIGHEST)
    gram_matrix = lax.psum(partial_gram, "fsdp")
    block_width = gathered.shape[2] // lax.axis_size("task")
    pieces = lax.dynamic_slice_in_dim(
        gathered, lax.axis_index("task") * block_width, block_width, 2
    )
    task_alpha = task_weights(gram_matrix)
    combined = jnp.einsum("t,tij->ij", task_alpha, pieces, precision=lax.Precision.HIGHEST)
    squared = lax.psum(jnp.sum(combined * combined), ("task", "fsdp"))
    grad_norm = jnp.sqrt(1e-06 + squared)
    clipped = combined * (math.sqrt(2 * RANK * D) / grad_norm)
    return adam(clipped, moment_one, moment_two)


def flip2(z, d):
    if d == 0:
        return z
    if d == 1:
        return z + 1 - 2 * (z % 2)
    if d == 2:
        return (z + 2) % 4
    return 3 - z


def kernel(
    ctx_hbm, cot_hbm, ada_hbm, out,
    ctx, cot,
    gathered, grad, core_in, x_in, z_in, z_far, y_in, gram_out, gram_in, gram_mid, gram_last,
    load, az_s, az_r, ax_s, ax_r, ay_s, ay_r, ac_s, ac_r,
    gc_s, gc_r, gx_s, gx_r, gz_s, gz_r, gy_s, gy_r, ka_s, ka_r, kz_s, kz_r,
):
    f32 = jnp.float32
    rows, width = ada_hbm.shape
    rank = width // 2
    half = rows // 2
    t = lax.axis_index("task")
    f = lax.axis_index("fsdp")
    c = f % 2
    x = (f // 2) % 2
    z = f // 4

    def place(z_, x_, c_):
        return (z_ * 2 + x_) * 2 + c_

    zpeer = {d: (t, place(flip2(z, d), x, c)) for d in (1, 2, 3)}
    xpeer = (t, place(z, 1 - x, c))
    cpeer = (t, place(z, x, 1 - c))
    cube = {
        k: (
            1 - t if k & 4 else t,
            place(z, 1 - x if k & 2 else x, 1 - c if k & 1 else c),
        )
        for k in range(1, 8)
    }

    def remote(src, dst, send, recv, peer):
        return pltpu.make_async_remote_copy(
            src_ref=src, dst_ref=dst, send_sem=send, recv_sem=recv, device_id=peer, device_id_type=MESH
        )

    loads = [
        pltpu.make_async_copy(ada_hbm, gathered.at[f], load.at[0]),
        pltpu.make_async_copy(ctx_hbm, ctx, load.at[1]),
        pltpu.make_async_copy(cot_hbm, cot, load.at[2]),
    ]
    for copy in loads:
        copy.start()
    barrier = pltpu.get_barrier_semaphore()
    for peer in list(zpeer.values()) + list(cube.values()):
        pl.semaphore_signal(barrier, inc=1, device_id=peer, device_id_type=MESH)
    pl.semaphore_wait(barrier, 10)

    sent = []

    def go(src, dst, send, recv, peer):
        copy = remote(src, dst, send, recv, peer)
        copy.start()
        sent.append(copy)

    near_half = pl.ds(pl.multiple_of(t * half, half), half)
    far_half = pl.ds(pl.multiple_of((1 - t) * half, half), half)
    whole = pl.ds(0, rows)
    ypeer = cube[4]

    def move_block(slot, part, send, recv, peer):
        go(gathered.at[slot, part, :], gathered.at[slot, part, :], send, recv, peer)

    def await_block(slot, part, send, recv, peer):
        ref = gathered.at[slot, part, :]
        remote(ref, ref, send, recv, peer).wait_recv()

    low = jnp.zeros((ctx.shape[0], rank), f32)
    back = jnp.zeros((ctx.shape[0], rank), f32)

    def columns(slot):
        return pl.ds(pl.multiple_of(slot * rows, rows), rows)

    def consume(slot, low, back):
        cols = columns(slot)
        low = low + jnp.dot(ctx[:, cols], gathered[slot, :, :rank], preferred_element_type=f32)
        back = back + jnp.dot(cot[:, cols], gathered[slot, :, rank:], preferred_element_type=f32)
        return low, back

    def line(d, far):
        return place(flip2(z, d), 1 - x if far else x, c)

    def to_other_core(slot, part, k):
        move_block(slot, part, ac_s.at[k], ac_r.at[k], cpeer)

    loads[0].wait()
    for d in (3, 2, 1):
        move_block(f, near_half, az_s.at[d], az_r.at[d], zpeer[d])
    move_block(f, whole, ax_s.at[0], ax_r.at[0], xpeer)
    to_other_core(f, whole, 0)
    loads[1].wait()
    loads[2].wait()
    low, back = consume(f, low, back)

    def from_z(d):
        slot = line(d, 0)
        await_block(slot, near_half, az_s.at[d], az_r.at[d], zpeer[d])
        move_block(slot, near_half, ax_s.at[d], ax_r.at[d], xpeer)
        move_block(slot, near_half, ay_s.at[d], ay_r.at[d], ypeer)
        to_other_core(slot, near_half, d)

    from_z(1)
    from_z(2)
    await_block(line(0, 1), whole, ax_s.at[0], ax_r.at[0], xpeer)
    to_other_core(line(0, 1), whole, 4)
    from_z(3)
    low, back = consume(line(0, 1), low, back)
    for d in (1, 2, 3):
        slot = line(d, 1)
        await_block(slot, near_half, ax_s.at[d], ax_r.at[d], xpeer)
        move_block(slot, near_half, ay_s.at[4 + d], ay_r.at[4 + d], ypeer)
        to_other_core(slot, near_half, 4 + d)
    for far in (0, 1):
        slot = place(z, 1 - x if far else x, 1 - c)
        await_block(slot, whole, ac_s.at[4 * far], ac_r.at[4 * far], cpeer)
        low, back = consume(slot, low, back)
    for far in (0, 1):
        for d in (1, 2, 3):
            k = 4 * far + d
            slot = line(d, far)
            await_block(slot, far_half, ay_s.at[k], ay_r.at[k], ypeer)
            to_other_core(slot, far_half, 8 + k)
            low, back = consume(slot, low, back)
    for far in (0, 1):
        for d in (1, 2, 3):
            k = 4 * far + d
            slot = place(flip2(z, d), 1 - x if far else x, 1 - c)
            await_block(slot, near_half, ac_s.at[k], ac_r.at[k], cpeer)
            await_block(slot, far_half, ac_s.at[8 + k], ac_r.at[8 + k], cpeer)
            low, back = consume(slot, low, back)

    low_t = low.T.astype(jnp.bfloat16)
    back_t = back.T.astype(jnp.bfloat16)

    quarter = rank // 2
    part_a = pl.ds(0, rank)
    part_u = pl.ds(rank, rank)
    part_b = pl.ds(rank, quarter)
    part_q = pl.ds(rank + quarter, quarter)
    rows_of = (part_a, part_b)

    def make(slot, u):
        cols = columns(slot)
        if u:
            grad[slot, part_u, :] = jnp.dot(low_t, cot[:, cols], preferred_element_type=f32)
        else:
            grad[slot, part_a, :] = jnp.dot(back_t, ctx[:, cols], preferred_element_type=f32)

    def to_core(d, far, u):
        slot = place(flip2(z, d), 1 - x if far else x, 1 - c)
        make(slot, u)
        k = 4 * far + d
        part = part_u if u else part_a
        go(grad.at[slot, part, :], core_in.at[k, part, :], gc_s.at[2 * k + u], gc_r.at[2 * k + u], cpeer)

    def keep(d, far, u):
        make(line(d, far), u)

    def add_core(d, far, u):
        slot = line(d, far)
        k = 4 * far + d
        part = part_u if u else part_a
        ref = core_in.at[k, part, :]
        remote(ref, ref, gc_s.at[2 * k + u], gc_r.at[2 * k + u], cpeer).wait_recv()
        grad[slot, part, :] = grad[slot, part, :] + core_in[k, part, :]

    def to_x(d, b):
        part = rows_of[b]
        go(grad.at[line(d, 1), part, :], x_in.at[d, part, :], gx_s.at[2 * d + b], gx_r.at[2 * d + b], xpeer)

    def from_x(d, b):
        part = rows_of[b]
        ref = x_in.at[d, part, :]
        remote(ref, ref, gx_s.at[2 * d + b], gx_r.at[2 * d + b], xpeer).wait_recv()
        grad[line(d, 0), part, :] = grad[line(d, 0), part, :] + x_in[d, part, :]

    def z_ref(m, chunk):
        if chunk == 3:
            return z_far.at[m]
        return z_in.at[m, (part_a, part_b, part_q)[chunk], :]

    def grad_ref(d, chunk):
        return grad.at[line(d, chunk == 3), (part_a, part_b, part_q, part_q)[chunk], :]

    def to_z(d, chunk):
        m = 0 if d == 3 else d
        n = 4 * m + chunk
        go(grad_ref(d, chunk), z_ref(m, chunk), gz_s.at[n], gz_r.at[n], zpeer[3 if d == 3 else 1])

    def from_z_sum(m, chunk):
        n = 4 * m + chunk
        ref = z_ref(m, chunk)
        remote(ref, ref, gz_s.at[n], gz_r.at[n], zpeer[1 if m else 3]).wait_recv()
        into = grad_ref(3 if m == 2 else 0, chunk)
        into[...] = into[...] + ref[...]

    to_core(2, 1, 0)
    keep(2, 1, 0)
    to_core(3, 1, 0)
    add_core(2, 1, 0)
    to_x(2, 0)
    keep(3, 1, 0)
    to_core(2, 1, 1)
    add_core(3, 1, 0)
    to_x(3, 0)
    keep(2, 1, 1)
    to_core(1, 1, 1)
    add_core(2, 1, 1)
    to_z(2, 3)
    to_x(2, 1)
    keep(1, 1, 1)
    to_core(2, 0, 1)
    add_core(1, 1, 1)
    keep(2, 0, 1)
    to_core(3, 1, 1)
    add_core(2, 0, 1)
    to_z(2, 2)
    to_z(1, 3)
    keep(3, 1, 1)
    to_core(1, 0, 1)
    add_core(3, 1, 1)
    to_x(3, 1)
    keep(1, 0, 1)
    to_core(1, 1, 0)
    add_core(1, 0, 1)
    to_z(1, 2)
    keep(1, 1, 0)
    to_core(2, 0, 0)
    add_core(1, 1, 0)
    to_x(1, 0)
    to_x(1, 1)
    keep(2, 0, 0)
    to_core(3, 0, 0)
    add_core(2, 0, 0)
    from_x(2, 0)
    to_z(2, 0)
    keep(3, 0, 0)
    to_core(3, 0, 1)
    keep(3, 0, 1)
    to_core(0, 1, 0)
    keep(0, 1, 0)
    to_core(0, 1, 1)
    add_core(0, 1, 0)
    to_x(0, 0)
    keep(0, 1, 1)
    add_core(3, 0, 0)
    add_core(3, 0, 1)
    add_core(0, 1, 1)
    to_x(0, 1)
    from_z_sum(2, 3)
    to_z(3, 3)
    from_z_sum(2, 2)
    to_z(3, 2)
    from_x(2, 1)
    to_z(2, 1)
    from_x(3, 0)
    to_core(1, 0, 0)
    keep(1, 0, 0)
    to_core(0, 0, 0)
    keep(0, 0, 0)
    to_core(0, 0, 1)
    keep(0, 0, 1)
    from_z_sum(2, 0)
    to_z(3, 0)
    add_core(1, 0, 0)
    add_core(0, 0, 0)
    add_core(0, 0, 1)
    from_x(3, 1)
    from_z_sum(2, 1)
    to_z(3, 1)
    from_x(1, 0)
    to_z(1, 0)
    from_z_sum(1, 3)
    from_z_sum(0, 3)
    go(grad_ref(0, 3), x_in.at[0, part_q, :], gx_s.at[8], gx_r.at[8], xpeer)
    from_x(1, 1)
    to_z(1, 1)
    from_z_sum(1, 2)
    from_z_sum(0, 2)
    for b in (0, 1):
        from_x(0, b)
    for m in (0, 1):
        for b in (0, 1):
            from_z_sum(m, b)
    remote(x_in.at[0, part_q, :], x_in.at[0, part_q, :], gx_s.at[8], gx_r.at[8], xpeer).wait_recv()
    grad[f, part_q, :] = grad[f, part_q, :] + x_in[0, part_q, :]
    mine = pl.ds(pl.multiple_of(t * rank, rank), rank)
    theirs = pl.ds(pl.multiple_of((1 - t) * rank, rank), rank)
    go(grad.at[f, theirs, :], y_in, gy_s, gy_r, cube[4])
    own = grad[f, mine, :]
    remote(y_in, y_in, gy_s, gy_r, cube[4]).wait_recv()
    other = y_in[...]

    first = t == 0
    own_sum = jnp.sum(own * own, axis=0, keepdims=True)
    both_sum = jnp.sum(own * other, axis=0, keepdims=True)
    other_sum = jnp.sum(other * other, axis=0, keepdims=True)
    rows_list = [jnp.where(first, own_sum, other_sum), both_sum, jnp.where(first, other_sum, own_sum)]
    gram_out[...] = jnp.zeros_like(gram_out)
    for k in range(3):
        total = rows_list[k]
        acc = total[:, :128]
        for j in range(1, rows // 128):
            acc = acc + total[:, j * 128 : (j + 1) * 128]
        gram_out[k : k + 1, :] = acc
    corner = (t * 2 + x) * 2 + c
    for k in range(1, 8):
        go(gram_out, gram_in.at[corner], ka_s.at[k], ka_r.at[k], cube[k])
    gram_in[corner] = gram_out[...]
    for k in range(1, 8):
        there = ((1 - t if k & 4 else t) * 2 + (1 - x if k & 2 else x)) * 2 + (1 - c if k & 1 else c)
        remote(gram_out, gram_in.at[there], ka_s.at[k], ka_r.at[k], cube[k]).wait_recv()
    gram_mid[...] = jnp.sum(gram_in[...], axis=0)
    for d in (3, 2, 1):
        go(gram_mid, gram_last.at[z], kz_s.at[d], kz_r.at[d], zpeer[d])
    gram_last[z] = gram_mid[...]
    for d in (3, 2, 1):
        remote(gram_mid, gram_last.at[flip2(z, d)], kz_s.at[d], kz_r.at[d], zpeer[d]).wait_recv()
    tile = jnp.sum(gram_last[...], axis=0)
    sums = jnp.sum(tile, axis=1, keepdims=True)
    k00, k01, k11 = sums[0:1], sums[1:2], sums[2:3]
    n0, n1 = jnp.sqrt(k00), jnp.sqrt(k11)
    right_side = k00 / n0 - k01 / n1
    system = (k00 - k01) / n0 - (k01 - k11) / n1
    alpha1 = right_side / system
    alpha0 = 1.0 - alpha1
    squared = alpha0 * alpha0 * k00 + 2.0 * alpha0 * alpha1 * k01 + alpha1 * alpha1 * k11
    scale = math.sqrt(2 * RANK * D) / jnp.sqrt(1e-06 + jnp.maximum(squared, 0.0))
    own_alpha = jnp.where(first, alpha0, alpha1) * scale
    other_alpha = jnp.where(first, alpha1, alpha0) * scale
    out[...] = (own * own_alpha + other * other_alpha).T
    for wait in sent:
        wait.wait_send()


def kernel_body(contexts, cotangents, adapter, moment_one, moment_two):
    rows, width = adapter.shape
    rank = width // 2
    f32 = jnp.float32
    dma = pltpu.SemaphoreType.DMA
    vmem = pl.BlockSpec(memory_space=pltpu.VMEM)
    clipped = pl.pallas_call(
        kernel,
        out_shape=jax.ShapeDtypeStruct((rows, rank), f32),
        in_specs=[pl.BlockSpec(memory_space=pltpu.HBM)] * 3,
        out_specs=vmem,
        scratch_shapes=[
            pltpu.VMEM(contexts.shape[1:], contexts.dtype),
            pltpu.VMEM(contexts.shape[1:], contexts.dtype),
            pltpu.VMEM((16, rows, width), adapter.dtype),
            pltpu.VMEM((16, width, rows), f32),
            pltpu.VMEM((8, width, rows), f32),
            pltpu.VMEM((4, width, rows), f32),
            pltpu.VMEM((3, width, rows), f32),
            pltpu.VMEM((3, rank // 2, rows), f32),
            pltpu.VMEM((rank, rows), f32),
            pltpu.VMEM((8, 128), f32),
            pltpu.VMEM((8, 8, 128), f32),
            pltpu.VMEM((8, 128), f32),
            pltpu.VMEM((4, 8, 128), f32),
            dma((3,)), dma((4,)), dma((4,)), dma((4,)), dma((4,)), dma((8,)), dma((8,)), dma((16,)), dma((16,)),
            dma((16,)), dma((16,)), dma((9,)), dma((9,)), dma((12,)), dma((12,)),
            dma, dma, dma((8,)), dma((8,)), dma((4,)), dma((4,)),
        ],
        compiler_params=pltpu.CompilerParams(
            collective_id=0, has_side_effects=True, vmem_limit_bytes=40 * 1024 * 1024
        ),
        name="grads_and_weights",
    )(contexts[0], cotangents[0], adapter)
    return adam(clipped, moment_one, moment_two)


def solution(mesh):
    in_specs = (
        P("task", "fsdp", None),
        P("task", "fsdp", None),
        P("fsdp", None),
        P("fsdp", "task"),
        P("fsdp", "task"),
    )
    out_specs = (P("fsdp", "task"), P("fsdp", "task"), P("fsdp", "task"))
    small = mesh.shape["task"] == 2 and mesh.shape["fsdp"] == 16
    body = kernel_body if small else general_body
    return jax.shard_map(body, mesh=mesh, in_specs=in_specs, out_specs=out_specs, check_vma=False)
```

```python
import math

import jax
import jax.numpy as jnp
from jax import lax
from jax.experimental import pallas as pl
from jax.experimental.pallas import tpu as pltpu
from jax.sharding import PartitionSpec as P

D = 4096
RANK = 128
MESH = pl.DeviceIdType.MESH


def eliminate(matrix, vector):
    extent = vector.shape[0]
    matrix_rows = [matrix[position] for position in range(extent)]
    values = [vector[position] for position in range(extent)]
    for column in range(extent):
        for target in range(column + 1, extent):
            factor = matrix_rows[target][column] / matrix_rows[column][column]
            matrix_rows[target] = matrix_rows[target] - factor * matrix_rows[column]
            values[target] = values[target] - factor * values[column]
    answer = [values[0] for position in range(extent)]
    for column in reversed(range(extent)):
        running = values[column]
        for follow in range(column + 1, extent):
            running = running - matrix_rows[column][follow] * answer[follow]
        answer[column] = running / matrix_rows[column][column]
    return jnp.stack(answer)


def task_weights(gram_matrix):
    task_norms = jnp.sqrt(jnp.diagonal(gram_matrix))
    right_side = gram_matrix[0, 0] / task_norms[0] - gram_matrix[0, 1:] / task_norms[1:]
    system = (gram_matrix[0, 0] - gram_matrix[1:, 0])[:, None] / task_norms[0] - (
        gram_matrix[0, 1:][None, :] - gram_matrix[1:, 1:]
    ) / task_norms[1:][None, :]
    solution = eliminate(system.T, right_side)
    return jnp.concatenate([jnp.reshape(1.0 - jnp.sum(solution), (1,)), solution])


def adam(clipped, moment_one, moment_two):
    first_moment = 0.9 * moment_one + 0.1 * clipped
    second_moment = 0.95 * moment_two + 0.05 * clipped * clipped
    adam_step = (
        first_moment / (1.0 - 0.9**20) / (jnp.sqrt(second_moment / (1.0 - 0.95**20)) + 1e-08)
    )
    return (first_moment, second_moment, adam_step)


def general_body(contexts, cotangents, adapter, moment_one, moment_two):
    own_context = contexts[0]
    own_cotangent = cotangents[0]
    rank_width = adapter.shape[1] // 2
    piece = lax.all_gather(adapter, "fsdp", axis=0, tiled=True)
    low = jnp.dot(own_context, piece[:, :rank_width], preferred_element_type=jnp.float32)
    back = jnp.dot(own_cotangent, piece[:, rank_width:], preferred_element_type=jnp.float32)
    low = low.astype(jnp.bfloat16)
    back = back.astype(jnp.bfloat16)
    over_tokens = (((0,), (0,)), ((), ()))
    down_part = lax.dot_general(own_context, back, over_tokens, preferred_element_type=jnp.float32)
    up_part = lax.dot_general(own_cotangent, low, over_tokens, preferred_element_type=jnp.float32)
    grad_rows = lax.psum_scatter(
        jnp.concatenate([down_part, up_part], axis=1), "fsdp", scatter_dimension=0, tiled=True
    )
    gathered = lax.all_gather(grad_rows[None], "task", axis=0, tiled=True)
    partial_gram = jnp.einsum("sij,tij->st", gathered, gathered, precision=lax.Precision.HIGHEST)
    gram_matrix = lax.psum(partial_gram, "fsdp")
    block_width = gathered.shape[2] // lax.axis_size("task")
    pieces = lax.dynamic_slice_in_dim(
        gathered, lax.axis_index("task") * block_width, block_width, 2
    )
    task_alpha = task_weights(gram_matrix)
    combined = jnp.einsum("t,tij->ij", task_alpha, pieces, precision=lax.Precision.HIGHEST)
    squared = lax.psum(jnp.sum(combined * combined), ("task", "fsdp"))
    grad_norm = jnp.sqrt(1e-06 + squared)
    clipped = combined * (math.sqrt(2 * RANK * D) / grad_norm)
    return adam(clipped, moment_one, moment_two)


def flip2(z, d):
    if d == 0:
        return z
    if d == 1:
        return z + 1 - 2 * (z % 2)
    if d == 2:
        return (z + 2) % 4
    return 3 - z


def kernel(
    ctx_hbm, cot_hbm, ada_hbm, out,
    ctx, cot,
    gathered, grad, core_in, x_in, z_in, z_far, y_in, gram_out, gram_in, gram_mid, gram_last,
    load, az_s, az_r, ax_s, ax_r, ay_s, ay_r, ac_s, ac_r,
    gc_s, gc_r, gx_s, gx_r, gz_s, gz_r, gy_s, gy_r, ka_s, ka_r, kz_s, kz_r,
):
    f32 = jnp.float32
    rows, width = ada_hbm.shape
    rank = width // 2
    half = rows // 2
    t = lax.axis_index("task")
    f = lax.axis_index("fsdp")
    c = f % 2
    x = (f // 2) % 2
    z = f // 4

    def place(z_, x_, c_):
        return (z_ * 2 + x_) * 2 + c_

    zpeer = {d: (t, place(flip2(z, d), x, c)) for d in (1, 2, 3)}
    xpeer = (t, place(z, 1 - x, c))
    cpeer = (t, place(z, x, 1 - c))
    cube = {
        k: (
            1 - t if k & 4 else t,
            place(z, 1 - x if k & 2 else x, 1 - c if k & 1 else c),
        )
        for k in range(1, 8)
    }

    def remote(src, dst, send, recv, peer):
        return pltpu.make_async_remote_copy(
            src_ref=src, dst_ref=dst, send_sem=send, recv_sem=recv, device_id=peer, device_id_type=MESH
        )

    loads = [
        pltpu.make_async_copy(ada_hbm, gathered.at[f], load.at[0]),
        pltpu.make_async_copy(ctx_hbm, ctx, load.at[1]),
        pltpu.make_async_copy(cot_hbm, cot, load.at[2]),
    ]
    for copy in loads:
        copy.start()
    barrier = pltpu.get_barrier_semaphore()
    for peer in list(zpeer.values()) + list(cube.values()):
        pl.semaphore_signal(barrier, inc=1, device_id=peer, device_id_type=MESH)
    pl.semaphore_wait(barrier, 10)

    sent = []

    def go(src, dst, send, recv, peer):
        copy = remote(src, dst, send, recv, peer)
        copy.start()
        sent.append(copy)

    near_half = pl.ds(pl.multiple_of(t * half, half), half)
    far_half = pl.ds(pl.multiple_of((1 - t) * half, half), half)
    whole = pl.ds(0, rows)
    ypeer = cube[4]

    def move_block(slot, part, send, recv, peer):
        go(gathered.at[slot, part, :], gathered.at[slot, part, :], send, recv, peer)

    def await_block(slot, part, send, recv, peer):
        ref = gathered.at[slot, part, :]
        remote(ref, ref, send, recv, peer).wait_recv()

    low = jnp.zeros((ctx.shape[0], rank), f32)
    back = jnp.zeros((ctx.shape[0], rank), f32)

    def columns(slot):
        return pl.ds(pl.multiple_of(slot * rows, rows), rows)

    def consume(slot, low, back):
        cols = columns(slot)
        low = low + jnp.dot(ctx[:, cols], gathered[slot, :, :rank], preferred_element_type=f32)
        back = back + jnp.dot(cot[:, cols], gathered[slot, :, rank:], preferred_element_type=f32)
        return low, back

    def line(d, far):
        return place(flip2(z, d), 1 - x if far else x, c)

    def to_other_core(slot, part, k):
        move_block(slot, part, ac_s.at[k], ac_r.at[k], cpeer)

    loads[0].wait()
    for d in (1, 2, 3):
        move_block(f, near_half, az_s.at[d], az_r.at[d], zpeer[d])
    move_block(f, whole, ax_s.at[0], ax_r.at[0], xpeer)
    to_other_core(f, whole, 0)
    loads[1].wait()
    loads[2].wait()
    low, back = consume(f, low, back)

    def from_z(d):
        slot = line(d, 0)
        await_block(slot, near_half, az_s.at[d], az_r.at[d], zpeer[d])
        move_block(slot, near_half, ax_s.at[d], ax_r.at[d], xpeer)
        move_block(slot, near_half, ay_s.at[d], ay_r.at[d], ypeer)
        to_other_core(slot, near_half, d)

    from_z(1)
    from_z(2)
    await_block(line(0, 1), whole, ax_s.at[0], ax_r.at[0], xpeer)
    to_other_core(line(0, 1), whole, 4)
    from_z(3)
    low, back = consume(line(0, 1), low, back)
    for d in (1, 2, 3):
        slot = line(d, 1)
        await_block(slot, near_half, ax_s.at[d], ax_r.at[d], xpeer)
        move_block(slot, near_half, ay_s.at[4 + d], ay_r.at[4 + d], ypeer)
        to_other_core(slot, near_half, 4 + d)
    for far in (0, 1):
        slot = place(z, 1 - x if far else x, 1 - c)
        await_block(slot, whole, ac_s.at[4 * far], ac_r.at[4 * far], cpeer)
        low, back = consume(slot, low, back)
    for far in (0, 1):
        for d in (1, 2, 3):
            k = 4 * far + d
            slot = line(d, far)
            await_block(slot, far_half, ay_s.at[k], ay_r.at[k], ypeer)
            to_other_core(slot, far_half, 8 + k)
            low, back = consume(slot, low, back)
    for far in (0, 1):
        for d in (1, 2, 3):
            k = 4 * far + d
            slot = place(flip2(z, d), 1 - x if far else x, 1 - c)
            await_block(slot, near_half, ac_s.at[k], ac_r.at[k], cpeer)
            await_block(slot, far_half, ac_s.at[8 + k], ac_r.at[8 + k], cpeer)
            low, back = consume(slot, low, back)

    low_t = low.T.astype(jnp.bfloat16)
    back_t = back.T.astype(jnp.bfloat16)

    quarter = rank // 2
    part_a = pl.ds(0, rank)
    part_u = pl.ds(rank, rank)
    part_b = pl.ds(rank, quarter)
    part_q = pl.ds(rank + quarter, quarter)
    rows_of = (part_a, part_b)

    def make(slot, u):
        cols = columns(slot)
        if u:
            grad[slot, part_u, :] = jnp.dot(low_t, cot[:, cols], preferred_element_type=f32)
        else:
            grad[slot, part_a, :] = jnp.dot(back_t, ctx[:, cols], preferred_element_type=f32)

    def to_core(d, far, u):
        slot = place(flip2(z, d), 1 - x if far else x, 1 - c)
        make(slot, u)
        k = 4 * far + d
        part = part_u if u else part_a
        go(grad.at[slot, part, :], core_in.at[k, part, :], gc_s.at[2 * k + u], gc_r.at[2 * k + u], cpeer)

    def keep(d, far, u):
        make(line(d, far), u)

    def add_core(d, far, u):
        slot = line(d, far)
        k = 4 * far + d
        part = part_u if u else part_a
        ref = core_in.at[k, part, :]
        remote(ref, ref, gc_s.at[2 * k + u], gc_r.at[2 * k + u], cpeer).wait_recv()
        grad[slot, part, :] = grad[slot, part, :] + core_in[k, part, :]

    def to_x(d, b):
        part = rows_of[b]
        go(grad.at[line(d, 1), part, :], x_in.at[d, part, :], gx_s.at[2 * d + b], gx_r.at[2 * d + b], xpeer)

    def from_x(d, b):
        part = rows_of[b]
        ref = x_in.at[d, part, :]
        remote(ref, ref, gx_s.at[2 * d + b], gx_r.at[2 * d + b], xpeer).wait_recv()
        grad[line(d, 0), part, :] = grad[line(d, 0), part, :] + x_in[d, part, :]

    def z_ref(m, chunk):
        if chunk == 3:
            return z_far.at[m]
        return z_in.at[m, (part_a, part_b, part_q)[chunk], :]

    def grad_ref(d, chunk):
        return grad.at[line(d, chunk == 3), (part_a, part_b, part_q, part_q)[chunk], :]

    def to_z(d, chunk):
        m = 0 if d == 3 else d
        n = 4 * m + chunk
        go(grad_ref(d, chunk), z_ref(m, chunk), gz_s.at[n], gz_r.at[n], zpeer[3 if d == 3 else 1])

    def from_z_sum(m, chunk):
        n = 4 * m + chunk
        ref = z_ref(m, chunk)
        remote(ref, ref, gz_s.at[n], gz_r.at[n], zpeer[1 if m else 3]).wait_recv()
        into = grad_ref(3 if m == 2 else 0, chunk)
        into[...] = into[...] + ref[...]

    to_core(2, 1, 0)
    keep(2, 1, 0)
    to_core(3, 1, 0)
    add_core(2, 1, 0)
    to_x(2, 0)
    keep(3, 1, 0)
    to_core(2, 1, 1)
    add_core(3, 1, 0)
    to_x(3, 0)
    keep(2, 1, 1)
    to_core(1, 1, 1)
    add_core(2, 1, 1)
    to_z(2, 3)
    to_x(2, 1)
    keep(1, 1, 1)
    to_core(2, 0, 1)
    add_core(1, 1, 1)
    keep(2, 0, 1)
    to_core(3, 1, 1)
    add_core(2, 0, 1)
    to_z(2, 2)
    to_z(1, 3)
    keep(3, 1, 1)
    to_core(1, 0, 1)
    add_core(3, 1, 1)
    to_x(3, 1)
    keep(1, 0, 1)
    to_core(1, 1, 0)
    add_core(1, 0, 1)
    to_z(1, 2)
    keep(1, 1, 0)
    to_core(2, 0, 0)
    add_core(1, 1, 0)
    to_x(1, 0)
    to_x(1, 1)
    keep(2, 0, 0)
    to_core(3, 0, 0)
    add_core(2, 0, 0)
    from_x(2, 0)
    to_z(2, 0)
    keep(3, 0, 0)
    to_core(3, 0, 1)
    keep(3, 0, 1)
    to_core(0, 1, 0)
    keep(0, 1, 0)
    to_core(0, 1, 1)
    add_core(0, 1, 0)
    to_x(0, 0)
    keep(0, 1, 1)
    add_core(3, 0, 0)
    add_core(3, 0, 1)
    add_core(0, 1, 1)
    to_x(0, 1)
    from_z_sum(2, 3)
    to_z(3, 3)
    from_z_sum(2, 2)
    to_z(3, 2)
    from_x(2, 1)
    to_z(2, 1)
    from_x(3, 0)
    to_core(1, 0, 0)
    keep(1, 0, 0)
    to_core(0, 0, 0)
    keep(0, 0, 0)
    to_core(0, 0, 1)
    keep(0, 0, 1)
    from_z_sum(2, 0)
    to_z(3, 0)
    add_core(1, 0, 0)
    add_core(0, 0, 0)
    add_core(0, 0, 1)
    from_x(3, 1)
    from_z_sum(2, 1)
    to_z(3, 1)
    from_x(1, 0)
    to_z(1, 0)
    from_z_sum(1, 3)
    from_z_sum(0, 3)
    go(grad_ref(0, 3), x_in.at[0, part_q, :], gx_s.at[8], gx_r.at[8], xpeer)
    from_x(1, 1)
    to_z(1, 1)
    from_z_sum(1, 2)
    from_z_sum(0, 2)
    for b in (0, 1):
        from_x(0, b)
    for m in (0, 1):
        for b in (0, 1):
            from_z_sum(m, b)
    remote(x_in.at[0, part_q, :], x_in.at[0, part_q, :], gx_s.at[8], gx_r.at[8], xpeer).wait_recv()
    grad[f, part_q, :] = grad[f, part_q, :] + x_in[0, part_q, :]
    mine = pl.ds(pl.multiple_of(t * rank, rank), rank)
    theirs = pl.ds(pl.multiple_of((1 - t) * rank, rank), rank)
    go(grad.at[f, theirs, :], y_in, gy_s, gy_r, cube[4])
    own = grad[f, mine, :]
    remote(y_in, y_in, gy_s, gy_r, cube[4]).wait_recv()
    other = y_in[...]

    first = t == 0
    own_sum = jnp.sum(own * own, axis=0, keepdims=True)
    both_sum = jnp.sum(own * other, axis=0, keepdims=True)
    other_sum = jnp.sum(other * other, axis=0, keepdims=True)
    rows_list = [jnp.where(first, own_sum, other_sum), both_sum, jnp.where(first, other_sum, own_sum)]
    gram_out[...] = jnp.zeros_like(gram_out)
    for k in range(3):
        total = rows_list[k]
        acc = total[:, :128]
        for j in range(1, rows // 128):
            acc = acc + total[:, j * 128 : (j + 1) * 128]
        gram_out[k : k + 1, :] = acc
    corner = (t * 2 + x) * 2 + c
    for k in range(1, 8):
        go(gram_out, gram_in.at[corner], ka_s.at[k], ka_r.at[k], cube[k])
    gram_in[corner] = gram_out[...]
    for k in range(1, 8):
        there = ((1 - t if k & 4 else t) * 2 + (1 - x if k & 2 else x)) * 2 + (1 - c if k & 1 else c)
        remote(gram_out, gram_in.at[there], ka_s.at[k], ka_r.at[k], cube[k]).wait_recv()
    gram_mid[...] = jnp.sum(gram_in[...], axis=0)
    for d in (3, 2, 1):
        go(gram_mid, gram_last.at[z], kz_s.at[d], kz_r.at[d], zpeer[d])
    gram_last[z] = gram_mid[...]
    for d in (3, 2, 1):
        remote(gram_mid, gram_last.at[flip2(z, d)], kz_s.at[d], kz_r.at[d], zpeer[d]).wait_recv()
    tile = jnp.sum(gram_last[...], axis=0)
    sums = jnp.sum(tile, axis=1, keepdims=True)
    k00, k01, k11 = sums[0:1], sums[1:2], sums[2:3]
    n0, n1 = jnp.sqrt(k00), jnp.sqrt(k11)
    right_side = k00 / n0 - k01 / n1
    system = (k00 - k01) / n0 - (k01 - k11) / n1
    alpha1 = right_side / system
    alpha0 = 1.0 - alpha1
    squared = alpha0 * alpha0 * k00 + 2.0 * alpha0 * alpha1 * k01 + alpha1 * alpha1 * k11
    scale = math.sqrt(2 * RANK * D) / jnp.sqrt(1e-06 + jnp.maximum(squared, 0.0))
    own_alpha = jnp.where(first, alpha0, alpha1) * scale
    other_alpha = jnp.where(first, alpha1, alpha0) * scale
    out[...] = (own * own_alpha + other * other_alpha).T
    for wait in sent:
        wait.wait_send()


def kernel_body(contexts, cotangents, adapter, moment_one, moment_two):
    rows, width = adapter.shape
    rank = width // 2
    f32 = jnp.float32
    dma = pltpu.SemaphoreType.DMA
    vmem = pl.BlockSpec(memory_space=pltpu.VMEM)
    clipped = pl.pallas_call(
        kernel,
        out_shape=jax.ShapeDtypeStruct((rows, rank), f32),
        in_specs=[pl.BlockSpec(memory_space=pltpu.HBM)] * 3,
        out_specs=vmem,
        scratch_shapes=[
            pltpu.VMEM(contexts.shape[1:], contexts.dtype),
            pltpu.VMEM(contexts.shape[1:], contexts.dtype),
            pltpu.VMEM((16, rows, width), adapter.dtype),
            pltpu.VMEM((16, width, rows), f32),
            pltpu.VMEM((8, width, rows), f32),
            pltpu.VMEM((4, width, rows), f32),
            pltpu.VMEM((3, width, rows), f32),
            pltpu.VMEM((3, rank // 2, rows), f32),
            pltpu.VMEM((rank, rows), f32),
            pltpu.VMEM((8, 128), f32),
            pltpu.VMEM((8, 8, 128), f32),
            pltpu.VMEM((8, 128), f32),
            pltpu.VMEM((4, 8, 128), f32),
            dma((3,)), dma((4,)), dma((4,)), dma((4,)), dma((4,)), dma((8,)), dma((8,)), dma((16,)), dma((16,)),
            dma((16,)), dma((16,)), dma((9,)), dma((9,)), dma((12,)), dma((12,)),
            dma, dma, dma((8,)), dma((8,)), dma((4,)), dma((4,)),
        ],
        compiler_params=pltpu.CompilerParams(
            collective_id=0, has_side_effects=True, vmem_limit_bytes=40 * 1024 * 1024
        ),
        name="grads_and_weights",
    )(contexts[0], cotangents[0], adapter)
    return adam(clipped, moment_one, moment_two)


def solution(mesh):
    in_specs = (
        P("task", "fsdp", None),
        P("task", "fsdp", None),
        P("fsdp", None),
        P("fsdp", "task"),
        P("fsdp", "task"),
    )
    out_specs = (P("fsdp", "task"), P("fsdp", "task"), P("fsdp", "task"))
    small = mesh.shape["task"] == 2 and mesh.shape["fsdp"] == 16
    body = kernel_body if small else general_body
    return jax.shard_map(body, mesh=mesh, in_specs=in_specs, out_specs=out_specs, check_vma=False)
```

```python
import math

import jax
import jax.numpy as jnp
from jax import lax
from jax.experimental import pallas as pl
from jax.experimental.pallas import tpu as pltpu
from jax.sharding import PartitionSpec as P

D = 4096
RANK = 128
MESH = pl.DeviceIdType.MESH


def eliminate(matrix, vector):
    extent = vector.shape[0]
    matrix_rows = [matrix[position] for position in range(extent)]
    values = [vector[position] for position in range(extent)]
    for column in range(extent):
        for target in range(column + 1, extent):
            factor = matrix_rows[target][column] / matrix_rows[column][column]
            matrix_rows[target] = matrix_rows[target] - factor * matrix_rows[column]
            values[target] = values[target] - factor * values[column]
    answer = [values[0] for position in range(extent)]
    for column in reversed(range(extent)):
        running = values[column]
        for follow in range(column + 1, extent):
            running = running - matrix_rows[column][follow] * answer[follow]
        answer[column] = running / matrix_rows[column][column]
    return jnp.stack(answer)


def task_weights(gram_matrix):
    task_norms = jnp.sqrt(jnp.diagonal(gram_matrix))
    right_side = gram_matrix[0, 0] / task_norms[0] - gram_matrix[0, 1:] / task_norms[1:]
    system = (gram_matrix[0, 0] - gram_matrix[1:, 0])[:, None] / task_norms[0] - (
        gram_matrix[0, 1:][None, :] - gram_matrix[1:, 1:]
    ) / task_norms[1:][None, :]
    solution = eliminate(system.T, right_side)
    return jnp.concatenate([jnp.reshape(1.0 - jnp.sum(solution), (1,)), solution])


def adam(clipped, moment_one, moment_two):
    first_moment = 0.9 * moment_one + 0.1 * clipped
    second_moment = 0.95 * moment_two + 0.05 * clipped * clipped
    adam_step = (
        first_moment / (1.0 - 0.9**20) / (jnp.sqrt(second_moment / (1.0 - 0.95**20)) + 1e-08)
    )
    return (first_moment, second_moment, adam_step)


def general_body(contexts, cotangents, adapter, moment_one, moment_two):
    own_context = contexts[0]
    own_cotangent = cotangents[0]
    rank_width = adapter.shape[1] // 2
    piece = lax.all_gather(adapter, "fsdp", axis=0, tiled=True)
    low = jnp.dot(own_context, piece[:, :rank_width], preferred_element_type=jnp.float32)
    back = jnp.dot(own_cotangent, piece[:, rank_width:], preferred_element_type=jnp.float32)
    low = low.astype(jnp.bfloat16)
    back = back.astype(jnp.bfloat16)
    over_tokens = (((0,), (0,)), ((), ()))
    down_part = lax.dot_general(own_context, back, over_tokens, preferred_element_type=jnp.float32)
    up_part = lax.dot_general(own_cotangent, low, over_tokens, preferred_element_type=jnp.float32)
    grad_rows = lax.psum_scatter(
        jnp.concatenate([down_part, up_part], axis=1), "fsdp", scatter_dimension=0, tiled=True
    )
    gathered = lax.all_gather(grad_rows[None], "task", axis=0, tiled=True)
    partial_gram = jnp.einsum("sij,tij->st", gathered, gathered, precision=lax.Precision.HIGHEST)
    gram_matrix = lax.psum(partial_gram, "fsdp")
    block_width = gathered.shape[2] // lax.axis_size("task")
    pieces = lax.dynamic_slice_in_dim(
        gathered, lax.axis_index("task") * block_width, block_width, 2
    )
    task_alpha = task_weights(gram_matrix)
    combined = jnp.einsum("t,tij->ij", task_alpha, pieces, precision=lax.Precision.HIGHEST)
    squared = lax.psum(jnp.sum(combined * combined), ("task", "fsdp"))
    grad_norm = jnp.sqrt(1e-06 + squared)
    clipped = combined * (math.sqrt(2 * RANK * D) / grad_norm)
    return adam(clipped, moment_one, moment_two)


def flip2(z, d):
    if d == 0:
        return z
    if d == 1:
        return z + 1 - 2 * (z % 2)
    if d == 2:
        return (z + 2) % 4
    return 3 - z


def kernel(
    ctx_hbm, cot_hbm, ada_hbm, out,
    ctx, cot,
    gathered, grad, core_in, x_in, z_in, z_far, y_in, gram_out, gram_in, gram_mid, gram_last,
    load, az_s, az_r, ax_s, ax_r, ay_s, ay_r, ac_s, ac_r,
    gc_s, gc_r, gx_s, gx_r, gz_s, gz_r, gy_s, gy_r, ka_s, ka_r, kz_s, kz_r,
):
    f32 = jnp.float32
    rows, width = ada_hbm.shape
    rank = width // 2
    half = rows // 2
    t = lax.axis_index("task")
    f = lax.axis_index("fsdp")
    c = f % 2
    x = (f // 2) % 2
    z = f // 4

    def place(z_, x_, c_):
        return (z_ * 2 + x_) * 2 + c_

    zpeer = {d: (t, place(flip2(z, d), x, c)) for d in (1, 2, 3)}
    xpeer = (t, place(z, 1 - x, c))
    cpeer = (t, place(z, x, 1 - c))
    cube = {
        k: (
            1 - t if k & 4 else t,
            place(z, 1 - x if k & 2 else x, 1 - c if k & 1 else c),
        )
        for k in range(1, 8)
    }

    def remote(src, dst, send, recv, peer):
        return pltpu.make_async_remote_copy(
            src_ref=src, dst_ref=dst, send_sem=send, recv_sem=recv, device_id=peer, device_id_type=MESH
        )

    loads = [
        pltpu.make_async_copy(ada_hbm, gathered.at[f], load.at[0]),
        pltpu.make_async_copy(ctx_hbm, ctx, load.at[1]),
        pltpu.make_async_copy(cot_hbm, cot, load.at[2]),
    ]
    for copy in loads:
        copy.start()
    barrier = pltpu.get_barrier_semaphore()
    for peer in list(zpeer.values()) + list(cube.values()):
        pl.semaphore_signal(barrier, inc=1, device_id=peer, device_id_type=MESH)
    pl.semaphore_wait(barrier, 10)

    sent = []

    def go(src, dst, send, recv, peer):
        copy = remote(src, dst, send, recv, peer)
        copy.start()
        sent.append(copy)

    near_half = pl.ds(pl.multiple_of(t * half, half), half)
    far_half = pl.ds(pl.multiple_of((1 - t) * half, half), half)
    whole = pl.ds(0, rows)
    ypeer = cube[4]

    def move_block(slot, part, send, recv, peer):
        go(gathered.at[slot, part, :], gathered.at[slot, part, :], send, recv, peer)

    def await_block(slot, part, send, recv, peer):
        ref = gathered.at[slot, part, :]
        remote(ref, ref, send, recv, peer).wait_recv()

    low = jnp.zeros((ctx.shape[0], rank), f32)
    back = jnp.zeros((ctx.shape[0], rank), f32)

    def columns(slot):
        return pl.ds(pl.multiple_of(slot * rows, rows), rows)

    def consume(slot, low, back):
        cols = columns(slot)
        low = low + jnp.dot(ctx[:, cols], gathered[slot, :, :rank], preferred_element_type=f32)
        back = back + jnp.dot(cot[:, cols], gathered[slot, :, rank:], preferred_element_type=f32)
        return low, back

    def line(d, far):
        return place(flip2(z, d), 1 - x if far else x, c)

    def to_other_core(slot, part, k):
        move_block(slot, part, ac_s.at[k], ac_r.at[k], cpeer)

    loads[0].wait()
    for d in (1, 2, 3):
        move_block(f, near_half, az_s.at[d], az_r.at[d], zpeer[d])
    move_block(f, whole, ax_s.at[0], ax_r.at[0], xpeer)
    to_other_core(f, whole, 0)
    loads[1].wait()
    loads[2].wait()
    low, back = consume(f, low, back)

    def from_z(d):
        slot = line(d, 0)
        await_block(slot, near_half, az_s.at[d], az_r.at[d], zpeer[d])
        move_block(slot, near_half, ax_s.at[d], ax_r.at[d], xpeer)
        move_block(slot, near_half, ay_s.at[d], ay_r.at[d], ypeer)
        to_other_core(slot, near_half, d)

    from_z(1)
    from_z(2)
    await_block(line(0, 1), whole, ax_s.at[0], ax_r.at[0], xpeer)
    to_other_core(line(0, 1), whole, 4)
    from_z(3)
    low, back = consume(line(0, 1), low, back)
    for d in (1, 2, 3):
        slot = line(d, 1)
        await_block(slot, near_half, ax_s.at[d], ax_r.at[d], xpeer)
        move_block(slot, near_half, ay_s.at[4 + d], ay_r.at[4 + d], ypeer)
        to_other_core(slot, near_half, 4 + d)
    for far in (0, 1):
        slot = place(z, 1 - x if far else x, 1 - c)
        await_block(slot, whole, ac_s.at[4 * far], ac_r.at[4 * far], cpeer)
        low, back = consume(slot, low, back)
    for far in (0, 1):
        for d in (1, 2, 3):
            k = 4 * far + d
            slot = line(d, far)
            await_block(slot, far_half, ay_s.at[k], ay_r.at[k], ypeer)
            to_other_core(slot, far_half, 8 + k)
    for far in (0, 1):
        for d in (1, 2, 3):
            low, back = consume(line(d, far), low, back)
    for far in (0, 1):
        for d in (1, 2, 3):
            k = 4 * far + d
            slot = place(flip2(z, d), 1 - x if far else x, 1 - c)
            await_block(slot, near_half, ac_s.at[k], ac_r.at[k], cpeer)
            await_block(slot, far_half, ac_s.at[8 + k], ac_r.at[8 + k], cpeer)
            low, back = consume(slot, low, back)

    low_t = low.T.astype(jnp.bfloat16)
    back_t = back.T.astype(jnp.bfloat16)

    quarter = rank // 2
    part_a = pl.ds(0, rank)
    part_u = pl.ds(rank, rank)
    part_b = pl.ds(rank, quarter)
    part_q = pl.ds(rank + quarter, quarter)
    rows_of = (part_a, part_b)

    def make(slot, u):
        cols = columns(slot)
        if u:
            grad[slot, part_u, :] = jnp.dot(low_t, cot[:, cols], preferred_element_type=f32)
        else:
            grad[slot, part_a, :] = jnp.dot(back_t, ctx[:, cols], preferred_element_type=f32)

    def to_core(d, far, u):
        slot = place(flip2(z, d), 1 - x if far else x, 1 - c)
        make(slot, u)
        k = 4 * far + d
        part = part_u if u else part_a
        go(grad.at[slot, part, :], core_in.at[k, part, :], gc_s.at[2 * k + u], gc_r.at[2 * k + u], cpeer)

    def keep(d, far, u):
        make(line(d, far), u)

    def add_core(d, far, u):
        slot = line(d, far)
        k = 4 * far + d
        part = part_u if u else part_a
        ref = core_in.at[k, part, :]
        remote(ref, ref, gc_s.at[2 * k + u], gc_r.at[2 * k + u], cpeer).wait_recv()
        grad[slot, part, :] = grad[slot, part, :] + core_in[k, part, :]

    def to_x(d, b):
        part = rows_of[b]
        go(grad.at[line(d, 1), part, :], x_in.at[d, part, :], gx_s.at[2 * d + b], gx_r.at[2 * d + b], xpeer)

    def from_x(d, b):
        part = rows_of[b]
        ref = x_in.at[d, part, :]
        remote(ref, ref, gx_s.at[2 * d + b], gx_r.at[2 * d + b], xpeer).wait_recv()
        grad[line(d, 0), part, :] = grad[line(d, 0), part, :] + x_in[d, part, :]

    def z_ref(m, chunk):
        if chunk == 3:
            return z_far.at[m]
        return z_in.at[m, (part_a, part_b, part_q)[chunk], :]

    def grad_ref(d, chunk):
        return grad.at[line(d, chunk == 3), (part_a, part_b, part_q, part_q)[chunk], :]

    def to_z(d, chunk):
        m = 0 if d == 3 else d
        n = 4 * m + chunk
        go(grad_ref(d, chunk), z_ref(m, chunk), gz_s.at[n], gz_r.at[n], zpeer[3 if d == 3 else 1])

    def from_z_sum(m, chunk):
        n = 4 * m + chunk
        ref = z_ref(m, chunk)
        remote(ref, ref, gz_s.at[n], gz_r.at[n], zpeer[1 if m else 3]).wait_recv()
        into = grad_ref(3 if m == 2 else 0, chunk)
        into[...] = into[...] + ref[...]

    to_core(2, 1, 0)
    keep(2, 1, 0)
    to_core(3, 1, 0)
    add_core(2, 1, 0)
    to_x(2, 0)
    keep(3, 1, 0)
    to_core(2, 1, 1)
    add_core(3, 1, 0)
    to_x(3, 0)
    keep(2, 1, 1)
    to_core(1, 1, 1)
    add_core(2, 1, 1)
    to_z(2, 3)
    to_x(2, 1)
    keep(1, 1, 1)
    to_core(2, 0, 1)
    add_core(1, 1, 1)
    keep(2, 0, 1)
    to_core(3, 1, 1)
    add_core(2, 0, 1)
    to_z(2, 2)
    to_z(1, 3)
    keep(3, 1, 1)
    to_core(1, 0, 1)
    add_core(3, 1, 1)
    to_x(3, 1)
    keep(1, 0, 1)
    to_core(1, 1, 0)
    add_core(1, 0, 1)
    to_z(1, 2)
    keep(1, 1, 0)
    to_core(2, 0, 0)
    add_core(1, 1, 0)
    to_x(1, 0)
    to_x(1, 1)
    keep(2, 0, 0)
    to_core(3, 0, 0)
    add_core(2, 0, 0)
    from_x(2, 0)
    to_z(2, 0)
    keep(3, 0, 0)
    to_core(3, 0, 1)
    keep(3, 0, 1)
    to_core(0, 1, 0)
    keep(0, 1, 0)
    to_core(0, 1, 1)
    add_core(0, 1, 0)
    to_x(0, 0)
    keep(0, 1, 1)
    add_core(3, 0, 0)
    add_core(3, 0, 1)
    add_core(0, 1, 1)
    to_x(0, 1)
    from_z_sum(2, 3)
    to_z(3, 3)
    from_z_sum(2, 2)
    to_z(3, 2)
    from_x(2, 1)
    to_z(2, 1)
    from_x(3, 0)
    to_core(1, 0, 0)
    keep(1, 0, 0)
    to_core(0, 0, 0)
    keep(0, 0, 0)
    to_core(0, 0, 1)
    keep(0, 0, 1)
    from_z_sum(2, 0)
    to_z(3, 0)
    add_core(1, 0, 0)
    add_core(0, 0, 0)
    add_core(0, 0, 1)
    from_x(3, 1)
    from_z_sum(2, 1)
    to_z(3, 1)
    from_x(1, 0)
    to_z(1, 0)
    from_z_sum(1, 3)
    from_z_sum(0, 3)
    go(grad_ref(0, 3), x_in.at[0, part_q, :], gx_s.at[8], gx_r.at[8], xpeer)
    from_x(1, 1)
    to_z(1, 1)
    from_z_sum(1, 2)
    from_z_sum(0, 2)
    for b in (0, 1):
        from_x(0, b)
    for m in (0, 1):
        for b in (0, 1):
            from_z_sum(m, b)
    remote(x_in.at[0, part_q, :], x_in.at[0, part_q, :], gx_s.at[8], gx_r.at[8], xpeer).wait_recv()
    grad[f, part_q, :] = grad[f, part_q, :] + x_in[0, part_q, :]
    mine = pl.ds(pl.multiple_of(t * rank, rank), rank)
    theirs = pl.ds(pl.multiple_of((1 - t) * rank, rank), rank)
    go(grad.at[f, theirs, :], y_in, gy_s, gy_r, cube[4])
    own = grad[f, mine, :]
    remote(y_in, y_in, gy_s, gy_r, cube[4]).wait_recv()
    other = y_in[...]

    first = t == 0
    own_sum = jnp.sum(own * own, axis=0, keepdims=True)
    both_sum = jnp.sum(own * other, axis=0, keepdims=True)
    other_sum = jnp.sum(other * other, axis=0, keepdims=True)
    rows_list = [jnp.where(first, own_sum, other_sum), both_sum, jnp.where(first, other_sum, own_sum)]
    gram_out[...] = jnp.zeros_like(gram_out)
    for k in range(3):
        total = rows_list[k]
        acc = total[:, :128]
        for j in range(1, rows // 128):
            acc = acc + total[:, j * 128 : (j + 1) * 128]
        gram_out[k : k + 1, :] = acc
    corner = (t * 2 + x) * 2 + c
    for k in range(1, 8):
        go(gram_out, gram_in.at[corner], ka_s.at[k], ka_r.at[k], cube[k])
    gram_in[corner] = gram_out[...]
    for k in range(1, 8):
        there = ((1 - t if k & 4 else t) * 2 + (1 - x if k & 2 else x)) * 2 + (1 - c if k & 1 else c)
        remote(gram_out, gram_in.at[there], ka_s.at[k], ka_r.at[k], cube[k]).wait_recv()
    gram_mid[...] = jnp.sum(gram_in[...], axis=0)
    for d in (3, 2, 1):
        go(gram_mid, gram_last.at[z], kz_s.at[d], kz_r.at[d], zpeer[d])
    gram_last[z] = gram_mid[...]
    for d in (3, 2, 1):
        remote(gram_mid, gram_last.at[flip2(z, d)], kz_s.at[d], kz_r.at[d], zpeer[d]).wait_recv()
    tile = jnp.sum(gram_last[...], axis=0)
    sums = jnp.sum(tile, axis=1, keepdims=True)
    k00, k01, k11 = sums[0:1], sums[1:2], sums[2:3]
    n0, n1 = jnp.sqrt(k00), jnp.sqrt(k11)
    right_side = k00 / n0 - k01 / n1
    system = (k00 - k01) / n0 - (k01 - k11) / n1
    alpha1 = right_side / system
    alpha0 = 1.0 - alpha1
    squared = alpha0 * alpha0 * k00 + 2.0 * alpha0 * alpha1 * k01 + alpha1 * alpha1 * k11
    scale = math.sqrt(2 * RANK * D) / jnp.sqrt(1e-06 + jnp.maximum(squared, 0.0))
    own_alpha = jnp.where(first, alpha0, alpha1) * scale
    other_alpha = jnp.where(first, alpha1, alpha0) * scale
    out[...] = (own * own_alpha + other * other_alpha).T
    for wait in sent:
        wait.wait_send()


def kernel_body(contexts, cotangents, adapter, moment_one, moment_two):
    rows, width = adapter.shape
    rank = width // 2
    f32 = jnp.float32
    dma = pltpu.SemaphoreType.DMA
    vmem = pl.BlockSpec(memory_space=pltpu.VMEM)
    clipped = pl.pallas_call(
        kernel,
        out_shape=jax.ShapeDtypeStruct((rows, rank), f32),
        in_specs=[pl.BlockSpec(memory_space=pltpu.HBM)] * 3,
        out_specs=vmem,
        scratch_shapes=[
            pltpu.VMEM(contexts.shape[1:], contexts.dtype),
            pltpu.VMEM(contexts.shape[1:], contexts.dtype),
            pltpu.VMEM((16, rows, width), adapter.dtype),
            pltpu.VMEM((16, width, rows), f32),
            pltpu.VMEM((8, width, rows), f32),
            pltpu.VMEM((4, width, rows), f32),
            pltpu.VMEM((3, width, rows), f32),
            pltpu.VMEM((3, rank // 2, rows), f32),
            pltpu.VMEM((rank, rows), f32),
            pltpu.VMEM((8, 128), f32),
            pltpu.VMEM((8, 8, 128), f32),
            pltpu.VMEM((8, 128), f32),
            pltpu.VMEM((4, 8, 128), f32),
            dma((3,)), dma((4,)), dma((4,)), dma((4,)), dma((4,)), dma((8,)), dma((8,)), dma((16,)), dma((16,)),
            dma((16,)), dma((16,)), dma((9,)), dma((9,)), dma((12,)), dma((12,)),
            dma, dma, dma((8,)), dma((8,)), dma((4,)), dma((4,)),
        ],
        compiler_params=pltpu.CompilerParams(
            collective_id=0, has_side_effects=True, vmem_limit_bytes=40 * 1024 * 1024
        ),
        name="grads_and_weights",
    )(contexts[0], cotangents[0], adapter)
    return adam(clipped, moment_one, moment_two)


def solution(mesh):
    in_specs = (
        P("task", "fsdp", None),
        P("task", "fsdp", None),
        P("fsdp", None),
        P("fsdp", "task"),
        P("fsdp", "task"),
    )
    out_specs = (P("fsdp", "task"), P("fsdp", "task"), P("fsdp", "task"))
    small = mesh.shape["task"] == 2 and mesh.shape["fsdp"] == 16
    body = kernel_body if small else general_body
    return jax.shard_map(body, mesh=mesh, in_specs=in_specs, out_specs=out_specs, check_vma=False)
```
